32 devices in a mesh: shard: 4 (over y, x), seq: 8 (over z, core).
Axes of the slice: x: 2, y: 2, z: 4, core: 2. Of those that a mesh axis runs over, the one named last changes fastest.
Arguments:
- queries: bfloat16 [64, 4096], P(('shard', 'seq')), may hold values from -25 to 25
- cached_keys: bfloat16 [8, 8192, 1024], P('shard', 'seq'), may hold values from -6 to 6
- cached_values: bfloat16 [8, 8192, 1024], P('shard', 'seq'), may hold values from -96 to 96
- shard_hits: int32 [64, 8], P(('shard', 'seq')), may hold values from 0 to 1, as said below
Outputs:
- attended: bfloat16 [64, 4096], P(('shard', 'seq'))
The draws below stay inside these ranges and needn't reach their ends.
Inputs may be any that keep to these rules, and one draw needn't show every extreme that they name: `shard_hits`: each query lists 1 to 4 of the 8 shards. At most 32 queries list any one shard, and some shard is listed by exactly 32.
All inputs are finite; a program needn't handle non-finite values.
Results may differ from the reference program's by a relative error of at most 0.0035.
Values may be sent and summed in bfloat16 or wider, within the bound.
No kernel may reach another device: no remote copies, remote signals or barrier semaphores. Data moves between devices by JAX's collectives and lax.ppermute only.
A program may use at most 128 MiB of HBM per device.

```python
import math
import jax
import jax.numpy as jnp
from jax import lax

KVH = 8
HD = 128
D = 4096
GROUP = 4
SHARDS = 8
QUERIES = 64
CAP = 32
CTX = 8192
KB = 512


def draw_cached_keys(key, part):
    key = jax.random.fold_in(key, 2)
    entries = jnp.clip(jax.random.normal(key, (SHARDS, CTX, KVH * HD), jnp.float32), -6.0, 6.0)
    return entries.astype(jnp.bfloat16)


def draw_queries(key, part):
    key = jax.random.fold_in(key, 3)
    first_key = jax.random.fold_in(key, 0)
    entries = jnp.clip(2.5 * jax.random.normal(first_key, (QUERIES, D), jnp.float32), -15.0, 15.0)
    return entries.astype(jnp.bfloat16)


def draw_shard_hits(key, part):
    key = jax.random.fold_in(key, 1)
    subkeys = jax.random.split(key, 5)
    hottest = jax.random.randint(subkeys[0], (), 0, SHARDS)
    ordering = jax.random.permutation(subkeys[1], QUERIES)
    ranking = jnp.zeros((QUERIES,), jnp.int32).at[ordering].set(jnp.arange(QUERIES, dtype=jnp.int32))
    shard_ids = jnp.arange(SHARDS, dtype=jnp.int32)
    lists_hot = ranking < CAP
    remaining = (hottest + 1 + jnp.arange(SHARDS - 1, dtype=jnp.int32)) % SHARDS
    first_pick = jnp.take(remaining, (ranking - CAP) % (SHARDS - 1))
    first_hit = (~lists_hot)[:, None] & (shard_ids[None, :] == first_pick[:, None])
    hot_hit = lists_hot[:, None] & (shard_ids[None, :] == hottest)
    favour = jax.random.permutation(subkeys[2], SHARDS).astype(jnp.int32)
    weight = jax.random.randint(subkeys[3], (QUERIES, SHARDS), 0, 256) + 64 * favour[None, :]
    priority = weight * 16 + shard_ids[None, :]
    eligible = ~first_hit & (shard_ids[None, :] != hottest)
    priority = jnp.where(eligible, priority, -1)
    _, best_ids = lax.top_k(priority, 3)
    extra_count = jax.random.randint(subkeys[4], (QUERIES,), 0, 4)
    extra_hit = jnp.zeros((QUERIES, SHARDS), bool)
    for depth in range(3):
        extra_hit = extra_hit | (shard_ids[None, :] == best_ids[:, depth:depth + 1]) & (depth < extra_count)[:, None]
    base_count = jnp.sum(first_hit.astype(jnp.int32), axis=0)
    running_count = jnp.cumsum(extra_hit.astype(jnp.int32), axis=0)
    kept_hit = extra_hit & (base_count[None, :] + running_count <= CAP)
    return (hot_hit | first_hit | kept_hit).astype(jnp.int32)


def level_of(rng, dims, shards, low, top_value):
    loudness = 1.0
    for axis_at, blocks in shards:
        draws = jax.random.uniform(jax.random.fold_in(jax.random.fold_in(rng, 6), axis_at), (blocks,), jnp.float32, low / len(shards), top_value / len(shards))
        loudness = loudness * jnp.repeat(jnp.exp(draws), dims[axis_at] // blocks).reshape((-1,) + (1,) * (len(dims) - 1 - axis_at))
    return loudness


def bell_draw(stream_key, extent, width, limit, pieces=(), kind=jnp.bfloat16):
    drawn = width * jax.random.normal(stream_key, extent, jnp.float32)
    if pieces:
        drawn = drawn * level_of(stream_key, extent, pieces, -0.22, 0.18)
    return jnp.clip(drawn, -limit, limit).astype(kind)


def setup_inputs(seed: int = 0) -> dict:
    key_of = jax.random.split(jax.random.key(seed), 5)
    queries = draw_queries(jax.random.fold_in(key_of[4], 71), 0)
    cached_keys = draw_cached_keys(jax.random.fold_in(key_of[4], 71), 0)
    cached_values = bell_draw(key_of[2], (SHARDS, CTX, KVH * HD), 16.0, 96.0, ((0, 4), (1, 8)))
    shard_hits = draw_shard_hits(jax.random.fold_in(key_of[4], 71), 0)
    return dict(queries=queries, cached_keys=cached_keys, cached_values=cached_values, shard_hits=shard_hits)


NEG_FILL = -1e+30

def combine_states(earlier, later):
    max_a, den_a, num_a = earlier
    max_b, den_b, num_b = later
    maximum = jnp.maximum(max_a, max_b)
    factor_a = jnp.exp(max_a - maximum)
    factor_b = jnp.exp(max_b - maximum)
    return (maximum, den_a * factor_a + den_b * factor_b, num_a * factor_a[..., None] + num_b * factor_b[..., None])

def reference(queries, cached_keys, cached_values, shard_hits):
    scale_factor = 1.0 / math.sqrt(HD)
    grouped = queries.astype(jnp.float32).reshape(QUERIES, KVH, GROUP, HD)
    blocks_per = CTX // KB
    key_blocks = cached_keys.reshape(SHARDS * blocks_per, KB, KVH, HD)
    value_blocks = cached_values.reshape(SHARDS * blocks_per, KB, KVH, HD)
    shard_of = (jnp.arange(SHARDS * blocks_per, dtype=jnp.int32) // blocks_per).astype(jnp.int32)

    def advance(running, block_pair):
        key_block, value_block, shard_id = block_pair
        scores = jnp.einsum('ngrd,tgd->ngrt', grouped, key_block.astype(jnp.float32)) * scale_factor
        block_peak = lax.optimization_barrier(jnp.max(scores, axis=-1))
        weights = jnp.exp(scores - block_peak[..., None]).astype(jnp.bfloat16)
        block_total = lax.optimization_barrier(jnp.sum(weights.astype(jnp.float32), axis=-1))
        block_value = jnp.einsum('ngrt,tgd->ngrd', weights.astype(jnp.float32), value_block.astype(jnp.float32))
        listed = lax.dynamic_index_in_dim(shard_hits, shard_id, 1, keepdims=False)
        is_listed = (listed > 0)[:, None, None]
        block_peak = jnp.where(is_listed, block_peak, NEG_FILL)
        block_total = jnp.where(is_listed, block_total, 0.0)
        block_value = jnp.where(is_listed[..., None], block_value, 0.0)
        return (combine_states(running, (block_peak, block_total, block_value)), None)
    start = (jnp.full((QUERIES, KVH, GROUP), NEG_FILL, jnp.float32), jnp.zeros((QUERIES, KVH, GROUP), jnp.float32), jnp.zeros((QUERIES, KVH, GROUP, HD), jnp.float32))
    final, _ = lax.scan(advance, start, (key_blocks, value_blocks, shard_of))
    merged = final[2] / final[1][..., None]
    return merged.reshape(QUERIES, D).astype(jnp.bfloat16)
```

```python
import functools
import math

import jax
import jax.numpy as jnp
from jax import lax
from jax.experimental import pallas as pl
from jax.experimental.pallas import tpu as pltpu
from jax.sharding import PartitionSpec as P

HD = 128
KB = 512
LANES = 128
NEG_FILL = -1e30
TO_LOG2 = math.log2(math.e) / math.sqrt(HD)
VMEM_LIMIT = 40 * 1024 * 1024
PART = 32


def params():
    return pltpu.CompilerParams(vmem_limit_bytes=VMEM_LIMIT)


def lane_iota(shape):
    return lax.broadcasted_iota(jnp.int32, shape, len(shape) - 1)


def pack_body(queries_ref, hits_ref, out_ref):
    own_rows, width = queries_ref.shape
    heads = width // HD
    chips, rows, _ = out_ref.shape
    group_rows = rows - 16 - heads * own_rows
    queries = queries_ref[...].astype(jnp.float32)
    pieces = [queries[:, h * HD:(h + 1) * HD] for h in range(heads)]
    hits = hits_ref[...].astype(jnp.float32)
    hits = jnp.concatenate(
        [hits, jnp.zeros((own_rows, LANES - hits.shape[1]), jnp.float32)], axis=1
    )
    pieces += [hits] * (16 // own_rows)
    message = jnp.concatenate(pieces, axis=0).astype(jnp.bfloat16)
    out_ref[...] = jnp.broadcast_to(message[None], out_ref.shape)


def pack(queries, hits, chips):
    own_rows, width = queries.shape
    rows = width // HD * own_rows + 16
    return pl.pallas_call(
        pack_body,
        out_shape=jax.ShapeDtypeStruct((chips, rows, LANES), jnp.bfloat16),
        compiler_params=params(),
        name="pack_queries",
    )(queries, hits)


def attend_body(kv_heads, q_ref, k_hbm, v_hbm, out_ref, q_buf, k_buf, v_buf, k_sem, v_sem):
    chips, msg_rows, _ = q_ref.shape
    slab = (msg_rows - 16) // kv_heads
    rows = chips * slab
    local_shards, positions, _ = k_hbm.shape
    blocks = positions // KB

    def copies(g):
        columns = pl.ds(g * HD, HD)
        return (
            pltpu.make_async_copy(k_hbm.at[:, :, columns], k_buf.at[g], k_sem.at[g]),
            pltpu.make_async_copy(v_hbm.at[:, :, columns], v_buf.at[g], v_sem.at[g]),
        )

    for g in range(kv_heads):
        for copy in copies(g):
            copy.start()

    for pair in range(kv_heads // 2):
        both = q_ref[:, pair * 2 * slab:(pair + 1) * 2 * slab, :].astype(jnp.float32)
        for i in range(2):
            part = both[:, i * slab:(i + 1) * slab, :].reshape(rows, HD)
            q_buf[pair * 2 + i] = part.astype(jnp.bfloat16)
    listed = q_ref[:, msg_rows - 16:, :].astype(jnp.float32)[:, :slab, :].reshape(rows, LANES)
    first = lax.axis_index("shard") * local_shards
    lane = lane_iota((rows, LANES))
    hit = [
        jnp.sum(jnp.where(lane == first + slot, listed, 0.0), axis=1, keepdims=True) > 0.0
        for slot in range(local_shards)
    ]
    out_ref[kv_heads] = jnp.zeros((rows, LANES), jnp.float32)
    ones = jnp.ones((KB, LANES), jnp.bfloat16)

    def head(g, carry):
        for copy in copies(g):
            copy.wait()
        query = q_buf[g]
        peaks, sums = [], []
        for slot in range(local_shards):
            for block in range(blocks):
                at = slice(block * KB, (block + 1) * KB)
                scores = lax.dot_general(
                    query, k_buf[g, slot, at, :], (((1,), (1,)), ((), ())),
                    preferred_element_type=jnp.float32,
                )
                peak = jnp.max(scores, axis=1, keepdims=True)
                weights = jnp.exp2((scores - peak) * TO_LOG2).astype(jnp.bfloat16)
                values = jnp.concatenate([v_buf[g, slot, at, :], ones], axis=1)
                sums.append(jnp.dot(weights, values, preferred_element_type=jnp.float32))
                peaks.append(jnp.where(hit[slot], peak * TO_LOG2, NEG_FILL))
        top = functools.reduce(jnp.maximum, peaks)
        merged = None
        for i, (peak, total) in enumerate(zip(peaks, sums)):
            factor = jnp.where(hit[i // blocks], jnp.exp2(peak - top), 0.0)
            term = total * factor
            merged = term if merged is None else merged + term
        out_ref[g] = merged[:, :HD]
        stats = out_ref[kv_heads]
        stats = jnp.where(lane == g, top, stats)
        out_ref[kv_heads] = jnp.where(lane == g + PART, merged[:, HD:], stats)
        return carry

    lax.fori_loop(0, kv_heads, head, 0)


def attend(message, keys, values, kv_heads):
    chips, msg_rows, _ = message.shape
    rows = chips * ((msg_rows - 16) // kv_heads)
    local_shards, positions, _ = keys.shape
    cache = pltpu.VMEM((kv_heads, local_shards, positions, HD), keys.dtype)
    return pl.pallas_call(
        functools.partial(attend_body, kv_heads),
        out_shape=jax.ShapeDtypeStruct((kv_heads + 1, rows, LANES), jnp.float32),
        in_specs=[
            pl.BlockSpec(memory_space=pltpu.VMEM),
            pl.BlockSpec(memory_space=pl.ANY),
            pl.BlockSpec(memory_space=pl.ANY),
        ],
        out_specs=pl.BlockSpec(memory_space=pltpu.VMEM),
        scratch_shapes=[
            pltpu.VMEM((kv_heads, rows, HD), jnp.bfloat16),
            cache,
            cache,
            pltpu.SemaphoreType.DMA((kv_heads,)),
            pltpu.SemaphoreType.DMA((kv_heads,)),
        ],
        compiler_params=params(),
        cost_estimate=pl.CostEstimate(
            flops=4 * rows * keys.size,
            bytes_accessed=2 * keys.size * 2,
            transcendentals=rows * keys.size // HD,
        ),
        name="attend",
    )(message, keys, values)


def merge_body(a_ref, b_ref, out_ref):
    kv_heads = a_ref.shape[0] - 1
    rows = a_ref.shape[1]
    chips, msg_rows, _ = out_ref.shape
    slab = rows // chips
    a_stats, b_stats = a_ref[kv_heads], b_ref[kv_heads]
    shift = LANES - PART
    a_total, b_total = pltpu.roll(a_stats, shift, 1), pltpu.roll(b_stats, shift, 1)
    top = jnp.maximum(a_stats, b_stats)
    a_factor, b_factor = jnp.exp2(a_stats - top), jnp.exp2(b_stats - top)
    total = a_total * a_factor + b_total * b_factor
    some = total > 0.0
    safe = jnp.where(some, total, 1.0)
    a_share = jnp.where(some, a_factor / safe, 0.0)
    b_share = jnp.where(some, b_factor / safe, 0.0)
    level = jnp.where(some, top + jnp.log2(safe), NEG_FILL)
    averages = [
        (a_ref[g] * a_share[:, g:g + 1] + b_ref[g] * b_share[:, g:g + 1]).reshape(
            chips, slab, HD
        )
        for g in range(kv_heads)
    ]
    for pair in range(kv_heads // 2):
        both = jnp.concatenate(averages[2 * pair:2 * pair + 2], axis=1)
        out_ref[:, pair * 2 * slab:(pair + 1) * 2 * slab, :] = both.astype(jnp.bfloat16)
    lane = lane_iota((rows, LANES))
    rest = jnp.where(lane < kv_heads, level, 0.0)
    packed = jnp.zeros_like(rest)
    for i in range(3):
        part = rest.astype(jnp.bfloat16).astype(jnp.float32)
        rest = rest - part
        packed = packed + (pltpu.roll(part, PART * i, 1) if i else part)
    packed = packed.reshape(chips, slab, LANES)
    packed = jnp.concatenate([packed] * (16 // slab), axis=1)
    out_ref[:, msg_rows - 16:, :] = packed.astype(jnp.bfloat16)


def merge(a, b, chips):
    kv_heads = a.shape[0] - 1
    msg_rows = kv_heads * (a.shape[1] // chips) + 16
    return pl.pallas_call(
        merge_body,
        out_shape=jax.ShapeDtypeStruct((chips, msg_rows, LANES), jnp.bfloat16),
        compiler_params=params(),
        name="merge_cores",
    )(a, b)


def finish_body(x_ref, out_ref):
    chips, msg_rows, _ = x_ref.shape
    own_rows, width = out_ref.shape
    slab = 8
    kv_heads = (msg_rows - 16) // slab
    stats = x_ref[:, msg_rows - 16:, :].astype(jnp.float32)[:, :slab, :]
    stats = stats.reshape(chips * slab, LANES)
    level = stats
    for i in (1, 2):
        level = level + pltpu.roll(stats, LANES - PART * i, 1)
    level = level.reshape(chips, slab, LANES)
    top = jnp.max(level, axis=0, keepdims=True)
    factor = jnp.exp2(level - top)
    share = factor / jnp.sum(factor, axis=0, keepdims=True)
    pieces = []
    for pair in range(kv_heads // 2):
        both = x_ref[:, pair * 2 * slab:(pair + 1) * 2 * slab, :].astype(jnp.float32)
        for i in range(2):
            g = 2 * pair + i
            part = both[:, i * slab:(i + 1) * slab, :] * share[:, :, g:g + 1]
            part = jnp.sum(part, axis=0)
            pieces += [
                part[r * own_rows:(r + 1) * own_rows, :] for r in range(slab // own_rows)
            ]
    out_ref[...] = jnp.concatenate(pieces, axis=1).astype(jnp.bfloat16)


def finish(received, own_rows, width):
    return pl.pallas_call(
        finish_body,
        out_shape=jax.ShapeDtypeStruct((own_rows, width), jnp.bfloat16),
        compiler_params=params(),
        name="finish",
    )(received)


def shards(devices, queries, cached_keys, cached_values, shard_hits):
    kv_heads = cached_keys.shape[2] // HD
    chips = devices // 2
    axes = ("shard", "seq")
    same_core = [[2 * i + core for i in range(chips)] for core in range(2)]
    siblings = [(i, i ^ 1) for i in range(devices)]
    message = pack(queries, shard_hits, chips)
    own = lax.all_to_all(message, axes, 0, 0, axis_index_groups=same_core)
    other = lax.ppermute(own, axes, siblings)
    own_state = attend(own, cached_keys, cached_values, kv_heads)
    other_state = attend(other, cached_keys, cached_values, kv_heads)
    sibling_state = lax.ppermute(other_state, axes, siblings)
    partial = merge(own_state, sibling_state, chips)
    received = lax.all_to_all(partial, axes, 0, 0, axis_index_groups=same_core)
    return finish(received, *queries.shape)


def solution(mesh):
    both = P(("shard", "seq"), None)
    cache = P("shard", "seq", None)
    return jax.shard_map(
        functools.partial(shards, mesh.size),
        mesh=mesh,
        in_specs=(both, cache, cache, both),
        out_specs=both,
        check_vma=False,
    )
```

```python
import functools
import math

import jax
import jax.numpy as jnp
from jax import lax
from jax.experimental import pallas as pl
from jax.experimental.pallas import tpu as pltpu
from jax.sharding import PartitionSpec as P

HD = 128
KB = 512
LANES = 128
NEG_FILL = -1e30
TO_LOG2 = math.log2(math.e) / math.sqrt(HD)
PACK_COST = 20_000_000_000
VMEM_LIMIT = 40 * 1024 * 1024
PART = 32
SLAB = 8


def params():
    return pltpu.CompilerParams(vmem_limit_bytes=VMEM_LIMIT)


def lane_iota(shape):
    return lax.broadcasted_iota(jnp.int32, shape, len(shape) - 1)


def pack_body(queries_ref, hits_ref, out_ref):
    own_rows, width = queries_ref.shape
    heads = width // HD
    queries = queries_ref[...].astype(jnp.float32)
    pieces = [queries[:, h * HD:(h + 1) * HD] for h in range(heads)]
    hits = hits_ref[...].astype(jnp.float32)
    hits = jnp.concatenate(
        [hits, jnp.zeros((own_rows, LANES - hits.shape[1]), jnp.float32)], axis=1
    )
    pieces += [hits] * (SLAB // own_rows)
    message = jnp.concatenate(pieces, axis=0).astype(jnp.bfloat16)
    out_ref[...] = jnp.broadcast_to(message[None], out_ref.shape)


def pack(queries, hits, chips):
    own_rows, width = queries.shape
    rows = width // HD * own_rows + SLAB
    return pl.pallas_call(
        pack_body,
        out_shape=jax.ShapeDtypeStruct((chips, rows, LANES), jnp.bfloat16),
        compiler_params=params(),
        cost_estimate=pl.CostEstimate(flops=PACK_COST, bytes_accessed=0, transcendentals=0),
        name="pack_queries",
    )(queries, hits)


def rows_of(ref, g, slab):
    chips = ref.shape[0]
    pair = ref[:, (g // 2) * 2 * slab:(g // 2 + 1) * 2 * slab, :].astype(jnp.float32)
    at = (g % 2) * slab
    return pair[:, at:at + slab, :].reshape(chips * slab, LANES)


def one_hot(condition):
    return jnp.where(condition, 1.0, 0.0).astype(jnp.bfloat16)


def two_parts(x):
    high = x.astype(jnp.bfloat16)
    return high, (x - high.astype(jnp.float32)).astype(jnp.bfloat16)


def attend_body(own_rows, own_ref, other_ref, k_ref, v_ref, own_out, other_out, q_buf, y_buf):
    chips, msg_rows, _ = own_ref.shape
    slab = SLAB
    kv_heads = msg_rows // slab - 1
    group = slab // own_rows
    rows = chips * slab
    local_shards, positions, _ = k_ref.shape
    blocks = positions // KB
    cap = 2 * chips * own_rows // 2
    packed = group * cap
    both = 2 * rows

    listed = jnp.concatenate(
        [
            ref[:, msg_rows - slab:, :].astype(jnp.float32).reshape(rows, LANES)
            for ref in (own_ref, other_ref)
        ],
        axis=0,
    )
    first = lax.axis_index("shard") * local_shards
    lane = lane_iota((both, LANES))
    slots = jnp.zeros((both, LANES), jnp.float32)
    for slot in range(local_shards):
        hit = jnp.sum(jnp.where(lane == first + slot, listed, 0.0), axis=1, keepdims=True)
        slots = jnp.where(lane == slot, hit, slots)

    def query_of(at):
        return lax.div(at, slab) * own_rows + lax.rem(at, own_rows)

    def head_of(at):
        return lax.div(lax.rem(at, slab), own_rows)

    row_query = query_of(lax.broadcasted_iota(jnp.int32, (both, both), 0))
    col_query = query_of(lax.broadcasted_iota(jnp.int32, (both, both), 1))
    earlier = one_hot(col_query < row_query)
    place = jnp.dot(earlier, slots.astype(jnp.bfloat16), preferred_element_type=jnp.float32)
    slots_t = jnp.transpose(slots)[:8]
    later = one_hot(row_query < col_query)
    place_t = jnp.dot(slots_t.astype(jnp.bfloat16), later, preferred_element_type=jnp.float32)

    def packed_key(at):
        return lax.div(at, cap), (lax.rem(at, cap) * group).astype(jnp.float32)

    pick_head, pick_place = packed_key(lax.broadcasted_iota(jnp.int32, (packed, both), 0))
    pick_from = head_of(lax.broadcasted_iota(jnp.int32, (packed, both), 1))
    back_head, back_place = packed_key(lax.broadcasted_iota(jnp.int32, (both, packed), 1))
    back_from = head_of(lax.broadcasted_iota(jnp.int32, (both, packed), 0))
    back = []
    queries = [
        jnp.concatenate([rows_of(own_ref, g, slab), rows_of(other_ref, g, slab)], axis=0)
        for g in range(kv_heads)
    ]
    queries = jnp.concatenate(queries, axis=1).astype(jnp.bfloat16)
    for slot in range(local_shards):
        pick = one_hot(
            (pick_head == pick_from)
            & (pick_place == place_t[slot:slot + 1])
            & (slots_t[slot:slot + 1] > 0.0)
        )
        q_buf[slot] = jnp.dot(pick, queries, preferred_element_type=jnp.float32).astype(
            jnp.bfloat16
        )
        back.append(
            one_hot(
                (back_head == back_from)
                & (back_place == place[:, slot:slot + 1])
                & (slots[:, slot:slot + 1] > 0.0)
            )
        )

    ones = jnp.ones((KB, LANES), jnp.bfloat16)
    peak_of = []
    for slot in range(local_shards):
        tops = []
        for g in range(kv_heads):
            columns = slice(g * HD, (g + 1) * HD)
            query = q_buf[slot, :, columns]
            peaks, sums = [], []
            for block in range(blocks):
                at = slice(block * KB, (block + 1) * KB)
                scores = lax.dot_general(
                    k_ref[slot, at, columns], query, (((1,), (1,)), ((), ())),
                    preferred_element_type=jnp.float32,
                )
                peak = jnp.max(scores, axis=0, keepdims=True)
                weights = jnp.exp2((scores - peak) * TO_LOG2).astype(jnp.bfloat16)
                values = jnp.concatenate([v_ref[slot, at, columns], ones], axis=1)
                sums.append(
                    lax.dot_general(
                        weights, values, (((0,), (0,)), ((), ())),
                        preferred_element_type=jnp.float32,
                    )
                )
                peaks.append(peak * TO_LOG2)
            top = functools.reduce(jnp.maximum, peaks)
            factors = [jnp.exp2(peak - top) for peak in peaks]
            factors.append(jnp.zeros((8 - len(factors), packed), jnp.float32))
            factors = jnp.transpose(jnp.concatenate(factors, axis=0))
            total = sum(part * factors[:, i:i + 1] for i, part in enumerate(sums))
            high, low = two_parts(total)
            y_buf[slot, g] = jnp.concatenate([high, low], axis=0)
            tops.append(top)
        rest = jnp.concatenate(tops + [jnp.zeros_like(tops[0])] * (16 - kv_heads), axis=0)
        parts = []
        for _ in range(3):
            part = rest.astype(jnp.bfloat16)
            parts.append(part)
            rest = rest - part.astype(jnp.float32)
        peak = lax.dot_general(
            jnp.concatenate([back[slot]] * 3, axis=1), jnp.concatenate(parts, axis=1),
            (((1,), (1,)), ((), ())), preferred_element_type=jnp.float32,
        )
        peak_of.append(jnp.where(slots[:, slot:slot + 1] > 0.0, peak, NEG_FILL))

    top = functools.reduce(jnp.maximum, peak_of)
    factor_of = [jnp.where(peak > NEG_FILL, jnp.exp2(peak - top), 0.0) for peak in peak_of]
    twice = [jnp.concatenate([one] * 2, axis=1) for one in back]
    stats = jnp.zeros((both, LANES), jnp.float32)
    for g in range(kv_heads):
        total = None
        for slot in range(local_shards):
            term = jnp.dot(twice[slot], y_buf[slot, g], preferred_element_type=jnp.float32)
            term = term * factor_of[slot][:, g:g + 1]
            total = term if total is None else total + term
        own_out[g] = total[:rows, :HD]
        other_out[g] = total[rows:, :HD]
        stats = jnp.where(lane == g, top[:, g:g + 1], stats)
        stats = jnp.where(lane == g + PART, total[:, HD:], stats)
    own_out[kv_heads] = stats[:rows]
    other_out[kv_heads] = stats[rows:]


def attend(own, other, keys, values, own_rows):
    chips, msg_rows, _ = own.shape
    kv_heads = msg_rows // SLAB - 1
    rows = chips * SLAB
    packed = SLAB // own_rows * chips * own_rows
    local_shards = keys.shape[0]
    state = jax.ShapeDtypeStruct((kv_heads + 1, rows, LANES), jnp.float32)
    return pl.pallas_call(
        functools.partial(attend_body, own_rows),
        out_shape=(state, state),
        scratch_shapes=[
            pltpu.VMEM((local_shards, packed, kv_heads * HD), jnp.bfloat16),
            pltpu.VMEM((local_shards, kv_heads, 2 * packed, 2 * LANES), jnp.bfloat16),
        ],
        compiler_params=params(),
        cost_estimate=pl.CostEstimate(
            flops=4 * packed * keys.size,
            bytes_accessed=2 * keys.size * 2,
            transcendentals=packed * keys.size // HD,
        ),
        name="attend",
    )(own, other, keys, values)


def merge_body(a_ref, b_ref, out_ref):
    kv_heads = a_ref.shape[0] - 1
    rows = a_ref.shape[1]
    chips, msg_rows, _ = out_ref.shape
    slab = rows // chips
    a_stats, b_stats = a_ref[kv_heads], b_ref[kv_heads]
    shift = LANES - PART
    a_total, b_total = pltpu.roll(a_stats, shift, 1), pltpu.roll(b_stats, shift, 1)
    top = jnp.maximum(a_stats, b_stats)
    a_factor, b_factor = jnp.exp2(a_stats - top), jnp.exp2(b_stats - top)
    total = a_total * a_factor + b_total * b_factor
    some = total > 0.0
    safe = jnp.where(some, total, 1.0)
    a_share = jnp.where(some, a_factor / safe, 0.0)
    b_share = jnp.where(some, b_factor / safe, 0.0)
    level = jnp.where(some, top + jnp.log2(safe), NEG_FILL)
    averages = [
        (a_ref[g] * a_share[:, g:g + 1] + b_ref[g] * b_share[:, g:g + 1]).reshape(
            chips, slab, HD
        )
        for g in range(kv_heads)
    ]
    for pair in range(kv_heads // 2):
        both = jnp.concatenate(averages[2 * pair:2 * pair + 2], axis=1)
        out_ref[:, pair * 2 * slab:(pair + 1) * 2 * slab, :] = both.astype(jnp.bfloat16)
    lane = lane_iota((rows, LANES))
    rest = jnp.where(lane < kv_heads, level, 0.0)
    packed = jnp.zeros_like(rest)
    for i in range(3):
        part = rest.astype(jnp.bfloat16).astype(jnp.float32)
        rest = rest - part
        packed = packed + (pltpu.roll(part, PART * i, 1) if i else part)
    out_ref[:, msg_rows - slab:, :] = packed.reshape(chips, slab, LANES).astype(jnp.bfloat16)


def merge(a, b, chips):
    kv_heads = a.shape[0] - 1
    msg_rows = (kv_heads + 1) * SLAB
    return pl.pallas_call(
        merge_body,
        out_shape=jax.ShapeDtypeStruct((chips, msg_rows, LANES), jnp.bfloat16),
        compiler_params=params(),
        name="merge_cores",
    )(a, b)


def finish_body(x_ref, out_ref):
    chips, msg_rows, _ = x_ref.shape
    own_rows, width = out_ref.shape
    slab = SLAB
    kv_heads = msg_rows // slab - 1
    stats = x_ref[:, msg_rows - slab:, :].astype(jnp.float32).reshape(chips * slab, LANES)
    level = stats
    for i in (1, 2):
        level = level + pltpu.roll(stats, LANES - PART * i, 1)
    level = level.reshape(chips, slab, LANES)
    top = jnp.max(level, axis=0, keepdims=True)
    factor = jnp.exp2(level - top)
    share = factor / jnp.sum(factor, axis=0, keepdims=True)
    pieces = []
    for pair in range(kv_heads // 2):
        both = x_ref[:, pair * 2 * slab:(pair + 1) * 2 * slab, :].astype(jnp.float32)
        for i in range(2):
            g = 2 * pair + i
            part = both[:, i * slab:(i + 1) * slab, :] * share[:, :, g:g + 1]
            part = jnp.sum(part, axis=0)
            pieces += [
                part[r * own_rows:(r + 1) * own_rows, :] for r in range(slab // own_rows)
            ]
    out_ref[...] = jnp.concatenate(pieces, axis=1).astype(jnp.bfloat16)


def finish(received, own_rows, width):
    return pl.pallas_call(
        finish_body,
        out_shape=jax.ShapeDtypeStruct((own_rows, width), jnp.bfloat16),
        compiler_params=params(),
        name="finish",
    )(received)


def shards(devices, queries, cached_keys, cached_values, shard_hits):
    chips = devices // 2
    axes = ("shard", "seq")
    same_core = [[2 * i + core for i in range(chips)] for core in range(2)]
    siblings = [(i, i ^ 1) for i in range(devices)]
    message = pack(queries, shard_hits, chips)
    own = lax.all_to_all(message, axes, 0, 0, axis_index_groups=same_core)
    other = lax.ppermute(own, axes, siblings)
    own_state, other_state = attend(own, other, cached_keys, cached_values, queries.shape[0])
    sibling_state = lax.ppermute(other_state, axes, siblings)
    partial = merge(own_state, sibling_state, chips)
    received = lax.all_to_all(partial, axes, 0, 0, axis_index_groups=same_core)
    return finish(received, *queries.shape)


def solution(mesh):
    both = P(("shard", "seq"), None)
    cache = P("shard", "seq", None)
    return jax.shard_map(
        functools.partial(shards, mesh.size),
        mesh=mesh,
        in_specs=(both, cache, cache, both),
        out_specs=both,
        check_vma=False,
    )
```

```python
import functools
import math

import jax
import jax.numpy as jnp
from jax import lax
from jax.experimental import pallas as pl
from jax.experimental.pallas import tpu as pltpu
from jax.sharding import PartitionSpec as P

HD = 128
KB = 512
LANES = 128
NEG_FILL = -1e30
TO_LOG2 = math.log2(math.e) / math.sqrt(HD)
PACK_COST = 20_000_000_000
VMEM_LIMIT = 24 * 1024 * 1024
PART = 32
SLAB = 8


def params():
    return pltpu.CompilerParams(vmem_limit_bytes=VMEM_LIMIT)


def lane_iota(shape):
    return lax.broadcasted_iota(jnp.int32, shape, len(shape) - 1)


def pack_body(queries_hbm, hits_hbm, out_ref, queries_buf, hits_buf, sems):
    copies = [
        pltpu.make_async_copy(queries_hbm, queries_buf, sems.at[0]),
        pltpu.make_async_copy(hits_hbm, hits_buf, sems.at[1]),
    ]
    for copy in copies:
        copy.start()
    for copy in copies:
        copy.wait()
    own_rows, width = queries_buf.shape
    heads = width // HD
    queries = queries_buf[...].astype(jnp.float32)
    pieces = [queries[:, h * HD:(h + 1) * HD] for h in range(heads)]
    hits = hits_buf[...].astype(jnp.float32)
    hits = jnp.concatenate(
        [hits, jnp.zeros((own_rows, LANES - hits.shape[1]), jnp.float32)], axis=1
    )
    slab = [hits] * (SLAB // own_rows)
    half = heads // 2
    messages = jnp.stack(
        [
            jnp.concatenate(pieces[core * half:(core + 1) * half] + slab, axis=0)
            for core in range(2)
        ]
    ).astype(jnp.bfloat16)
    out_ref[...] = jnp.broadcast_to(messages[None], out_ref.shape)


def pack(queries, hits, devices):
    own_rows, width = queries.shape
    rows = width // HD // 2 * own_rows + SLAB
    out = pl.pallas_call(
        pack_body,
        out_shape=jax.ShapeDtypeStruct((devices // 2, 2, rows, LANES), jnp.bfloat16),
        in_specs=[pl.BlockSpec(memory_space=pltpu.HBM)] * 2,
        scratch_shapes=[
            pltpu.VMEM(queries.shape, queries.dtype),
            pltpu.VMEM(hits.shape, hits.dtype),
            pltpu.SemaphoreType.DMA((2,)),
        ],
        compiler_params=params(),
        cost_estimate=pl.CostEstimate(flops=PACK_COST, bytes_accessed=0, transcendentals=0),
        name="pack_queries",
    )(queries, hits)
    return out.reshape(devices, rows, LANES)


def rows_of(ref, g, slab):
    chips = ref.shape[0]
    pair = ref[:, (g // 2) * 2 * slab:(g // 2 + 1) * 2 * slab, :].astype(jnp.float32)
    at = (g % 2) * slab
    return pair[:, at:at + slab, :].reshape(chips * slab, LANES)


def one_hot(condition):
    return jnp.where(condition, 1.0, 0.0).astype(jnp.bfloat16)


def two_parts(x):
    high = x.astype(jnp.bfloat16)
    return high, (x - high.astype(jnp.float32)).astype(jnp.bfloat16)


def attend_body(own_rows, x_ref, *refs):
    *caches, out_ref, q_buf, y_buf = refs
    devices, msg_rows, _ = x_ref.shape
    slab = SLAB
    kv_heads = msg_rows // slab - 1
    group = slab // own_rows
    local_shards, positions, _ = caches[0].shape
    blocks = positions // KB
    cap = devices * own_rows // 2
    packed = group * cap
    both = devices * slab
    first_column = lax.rem(lax.axis_index("seq"), 2) * (kv_heads * HD)

    listed = x_ref[:, msg_rows - slab:, :].astype(jnp.float32).reshape(both, LANES)
    first = lax.axis_index("shard") * local_shards
    lane = lane_iota((both, LANES))
    slots = jnp.zeros((both, LANES), jnp.float32)
    for slot in range(local_shards):
        hit = jnp.sum(jnp.where(lane == first + slot, listed, 0.0), axis=1, keepdims=True)
        slots = jnp.where(lane == slot, hit, slots)

    def query_of(at):
        return lax.div(at, slab) * own_rows + lax.rem(at, own_rows)

    def head_of(at):
        return lax.div(lax.rem(at, slab), own_rows)

    row_query = query_of(lax.broadcasted_iota(jnp.int32, (both, both), 0))
    col_query = query_of(lax.broadcasted_iota(jnp.int32, (both, both), 1))
    earlier = one_hot(col_query < row_query)
    place = jnp.dot(earlier, slots.astype(jnp.bfloat16), preferred_element_type=jnp.float32)
    slots_t = jnp.transpose(slots)[:8]
    later = one_hot(row_query < col_query)
    place_t = jnp.dot(slots_t.astype(jnp.bfloat16), later, preferred_element_type=jnp.float32)

    def packed_key(at):
        return lax.div(at, cap), (lax.rem(at, cap) * group).astype(jnp.float32)

    pick_head, pick_place = packed_key(lax.broadcasted_iota(jnp.int32, (packed, both), 0))
    pick_from = head_of(lax.broadcasted_iota(jnp.int32, (packed, both), 1))
    back_head, back_place = packed_key(lax.broadcasted_iota(jnp.int32, (both, packed), 1))
    back_from = head_of(lax.broadcasted_iota(jnp.int32, (both, packed), 0))
    back = []
    queries = [rows_of(x_ref, g, slab) for g in range(kv_heads)]
    queries = jnp.concatenate(queries, axis=1).astype(jnp.bfloat16)
    for slot in range(local_shards):
        pick = one_hot(
            (pick_head == pick_from)
            & (pick_place == place_t[slot:slot + 1])
            & (slots_t[slot:slot + 1] > 0.0)
        )
        q_buf[slot] = jnp.dot(pick, queries, preferred_element_type=jnp.float32).astype(
            jnp.bfloat16
        )
        back.append(
            one_hot(
                (back_head == back_from)
                & (back_place == place[:, slot:slot + 1])
                & (slots[:, slot:slot + 1] > 0.0)
            )
        )

    ones = jnp.ones((KB, LANES), jnp.bfloat16)
    peak_of = []
    for slot in range(local_shards):
        tops = []
        for g in range(kv_heads):
            columns = pl.ds(pl.multiple_of(first_column + g * HD, HD), HD)
            query = q_buf[slot, :, g * HD:(g + 1) * HD]
            peaks, sums = [], []
            for block in range(2 * blocks):
                k_ref, v_ref = caches[2 * (block // blocks):2 * (block // blocks) + 2]
                at = slice(block % blocks * KB, (block % blocks + 1) * KB)
                scores = lax.dot_general(
                    k_ref[slot, at, columns], query, (((1,), (1,)), ((), ())),
                    preferred_element_type=jnp.float32,
                )
                peak = jnp.max(scores, axis=0, keepdims=True)
                weights = jnp.exp2((scores - peak) * TO_LOG2).astype(jnp.bfloat16)
                values = jnp.concatenate([v_ref[slot, at, columns], ones], axis=1)
                sums.append(
                    lax.dot_general(
                        weights, values, (((0,), (0,)), ((), ())),
                        preferred_element_type=jnp.float32,
                    )
                )
                peaks.append(peak * TO_LOG2)
            top = functools.reduce(jnp.maximum, peaks)
            factors = [jnp.exp2(peak - top) for peak in peaks]
            factors.append(jnp.zeros((8 - len(factors), packed), jnp.float32))
            factors = jnp.transpose(jnp.concatenate(factors, axis=0))
            total = sum(part * factors[:, i:i + 1] for i, part in enumerate(sums))
            high, low = two_parts(total)
            y_buf[slot, g] = jnp.concatenate([high, low], axis=0)
            tops.append(top)
        rest = jnp.concatenate(tops + [jnp.zeros_like(tops[0])] * (16 - kv_heads), axis=0)
        parts = []
        for _ in range(3):
            part = rest.astype(jnp.bfloat16)
            parts.append(part)
            rest = rest - part.astype(jnp.float32)
        peak = lax.dot_general(
            jnp.concatenate([back[slot]] * 3, axis=1), jnp.concatenate(parts, axis=1),
            (((1,), (1,)), ((), ())), preferred_element_type=jnp.float32,
        )
        peak_of.append(jnp.where(slots[:, slot:slot + 1] > 0.0, peak, NEG_FILL))

    top = functools.reduce(jnp.maximum, peak_of)
    factor_of = [jnp.where(peak > NEG_FILL, jnp.exp2(peak - top), 0.0) for peak in peak_of]
    twice = [jnp.concatenate([one] * 2, axis=1) for one in back]
    averages = []
    level = jnp.zeros((both, LANES), jnp.float32)
    for g in range(kv_heads):
        total = None
        for slot in range(local_shards):
            term = jnp.dot(twice[slot], y_buf[slot, g], preferred_element_type=jnp.float32)
            term = term * factor_of[slot][:, g:g + 1]
            total = term if total is None else total + term
        some = total[:, HD:] > 0.0
        safe = jnp.where(some, total[:, HD:], 1.0)
        averages.append((total[:, :HD] / safe).reshape(devices, slab, HD))
        weight = jnp.where(some, top[:, g:g + 1] + jnp.log2(safe), NEG_FILL)
        level = jnp.where(lane == g, weight, level)
    for pair in range(kv_heads // 2):
        out_ref[:, pair * 2 * slab:(pair + 1) * 2 * slab, :] = jnp.concatenate(
            averages[2 * pair:2 * pair + 2], axis=1
        ).astype(jnp.bfloat16)
    stats = jnp.zeros_like(level)
    for i in range(3):
        part = level.astype(jnp.bfloat16).astype(jnp.float32)
        level = level - part
        stats = stats + (pltpu.roll(part, PART * i, 1) if i else part)
    out_ref[:, msg_rows - slab:, :] = stats.reshape(devices, slab, LANES).astype(jnp.bfloat16)


def attend(message, caches, own_rows):
    devices, msg_rows, _ = message.shape
    kv_heads = msg_rows // SLAB - 1
    packed = SLAB * devices // 2
    keys = caches[0]
    local_shards = keys.shape[0]
    return pl.pallas_call(
        functools.partial(attend_body, own_rows),
        out_shape=jax.ShapeDtypeStruct(message.shape, jnp.bfloat16),
        scratch_shapes=[
            pltpu.VMEM((local_shards, packed, kv_heads * HD), jnp.bfloat16),
            pltpu.VMEM((local_shards, kv_heads, 2 * packed, 2 * LANES), jnp.bfloat16),
        ],
        compiler_params=params(),
        cost_estimate=pl.CostEstimate(
            flops=4 * packed * keys.size,
            bytes_accessed=4 * keys.size,
            transcendentals=packed * keys.size // HD,
        ),
        name="attend",
    )(message, *caches)


def finish_body(x_ref, out_ref):
    devices, msg_rows, _ = x_ref.shape
    own_rows, width = out_ref.shape
    slab = SLAB
    kv_heads = msg_rows // slab - 1
    stats = x_ref[:, msg_rows - slab:, :].astype(jnp.float32).reshape(devices * slab, LANES)
    level = stats
    for i in (1, 2):
        level = level + pltpu.roll(stats, LANES - PART * i, 1)
    level = level.reshape(devices // 2, 2, slab, LANES)
    top = jnp.max(level, axis=0, keepdims=True)
    factor = jnp.exp2(level - top)
    share = factor / jnp.sum(factor, axis=0, keepdims=True)
    pieces = []
    for core in range(2):
        for pair in range(kv_heads // 2):
            at = slice(pair * 2 * slab, (pair + 1) * 2 * slab)
            both = x_ref[:, at, :].astype(jnp.float32)
            both = both.reshape(devices // 2, 2, 2 * slab, LANES)[:, core]
            for i in range(2):
                g = 2 * pair + i
                part = both[:, i * slab:(i + 1) * slab, :] * share[:, core, :, g:g + 1]
                part = jnp.sum(part, axis=0)
                pieces += [
                    part[r * own_rows:(r + 1) * own_rows, :] for r in range(slab // own_rows)
                ]
    out_ref[...] = jnp.concatenate(pieces, axis=1).astype(jnp.bfloat16)


def finish(received, own_rows, width):
    return pl.pallas_call(
        finish_body,
        out_shape=jax.ShapeDtypeStruct((own_rows, width), jnp.bfloat16),
        compiler_params=params(),
        name="finish",
    )(received)


def shards(devices, queries, cached_keys, cached_values, shard_hits):
    axes = ("shard", "seq")
    siblings = [(i, i ^ 1) for i in range(devices)]
    caches = (
        cached_keys,
        cached_values,
        lax.ppermute(cached_keys, axes, siblings),
        lax.ppermute(cached_values, axes, siblings),
    )
    message = pack(queries, shard_hits, devices)
    received = lax.all_to_all(message, axes, 0, 0)
    partial = attend(received, caches, queries.shape[0])
    received = lax.all_to_all(partial, axes, 0, 0)
    return finish(received, *queries.shape)


def solution(mesh):
    both = P(("shard", "seq"), None)
    cache = P("shard", "seq", None)
    return jax.shard_map(
        functools.partial(shards, mesh.size),
        mesh=mesh,
        in_specs=(both, cache, cache, both),
        out_specs=both,
        check_vma=False,
    )
```

```python
import functools
import math

import jax
import jax.numpy as jnp
from jax import lax
from jax.experimental import pallas as pl
from jax.experimental.pallas import tpu as pltpu
from jax.sharding import PartitionSpec as P

HD = 128
KB = 512
LANES = 128
NEG_FILL = -1e30
TO_LOG2 = math.log2(math.e) / math.sqrt(HD)
PACK_COST = 20_000_000_000
VMEM_LIMIT = 24 * 1024 * 1024
PART = 32
SUBLANES = 8


def params():
    return pltpu.CompilerParams(vmem_limit_bytes=VMEM_LIMIT)


def lane_iota(shape):
    return lax.broadcasted_iota(jnp.int32, shape, len(shape) - 1)


def one_hot(condition):
    return jnp.where(condition, 1.0, 0.0).astype(jnp.bfloat16)


def dot(a, b):
    return jnp.dot(a, b, preferred_element_type=jnp.float32)


def parts_of(x, count):
    parts = []
    for _ in range(count):
        part = x.astype(jnp.bfloat16)
        parts.append(part)
        x = x - part.astype(jnp.float32)
    return parts


def pack_body(x_ref, out_ref):
    half = (x_ref.shape[1] - LANES) // 2
    x = x_ref[...]
    for core in range(2):
        message = jnp.concatenate([x[:, core * half:(core + 1) * half], x[:, 2 * half:]], axis=1)
        out_ref[:, core] = jnp.broadcast_to(message[None], (out_ref.shape[0],) + message.shape)


def pack(queries, hits, devices):
    own_rows, width = queries.shape
    hits = jnp.pad(hits.astype(jnp.bfloat16), ((0, 0), (0, LANES - hits.shape[1])))
    shape = (devices // 2, 2, own_rows, width // 2 + LANES)
    out = pl.pallas_call(
        pack_body,
        out_shape=jax.ShapeDtypeStruct(shape, jnp.bfloat16),
        compiler_params=params(),
        cost_estimate=pl.CostEstimate(flops=PACK_COST, bytes_accessed=0, transcendentals=0),
        name="pack_queries",
    )(jnp.concatenate([queries, hits], axis=1))
    return out.reshape(devices, own_rows, width // 2 + LANES)


def attend_body(x_ref, *refs):
    *caches, out_ref, q_buf, y_buf = refs
    devices, own_rows, message = x_ref.shape
    width = message - LANES
    heads = width // HD
    local_shards, positions, cache_width = caches[0].shape
    kv_heads = cache_width // HD // 2
    group = heads // kv_heads
    blocks = positions // KB
    rows = devices * own_rows
    cap = rows // 2
    packed = group * cap
    first_column = lax.rem(lax.axis_index("seq"), 2) * (kv_heads * HD)

    x = x_ref[...].reshape(rows, message)
    listed = x[:, width:].astype(jnp.float32)
    first = lax.axis_index("shard") * local_shards
    lane = lane_iota((rows, LANES))
    slots = jnp.zeros((rows, LANES), jnp.float32)
    for slot in range(local_shards):
        hit = jnp.sum(jnp.where(lane == first + slot, listed, 0.0), axis=1, keepdims=True)
        slots = jnp.where(lane == slot, hit, slots)
    hits = [slots[:, slot:slot + 1] > 0.0 for slot in range(local_shards)]
    row = lax.broadcasted_iota(jnp.int32, (rows, rows), 0)
    column = lax.broadcasted_iota(jnp.int32, (rows, rows), 1)
    place = dot(one_hot(column < row), slots.astype(jnp.bfloat16))
    slots_t = jnp.transpose(slots)[:SUBLANES]
    place_t = dot(slots_t.astype(jnp.bfloat16), one_hot(row < column))

    pick_at = lax.broadcasted_iota(jnp.int32, (cap, rows), 0).astype(jnp.float32)
    picks, backs = [], []
    for slot in range(local_shards):
        picks.append(
            one_hot((pick_at == place_t[slot:slot + 1]) & (slots_t[slot:slot + 1] > 0.0))
        )
        q_buf[slot] = dot(picks[slot], x[:, :width]).astype(jnp.bfloat16)
        back_at = lax.rem(lane_iota((rows, 3 * cap)), cap).astype(jnp.float32)
        backs.append(one_hot((back_at == place[:, slot:slot + 1]) & hits[slot]))

    ones = jnp.ones((KB, LANES), jnp.bfloat16)
    cap_lane = lane_iota((cap, LANES))
    levels = []
    for slot in range(local_shards):
        level = jnp.zeros((cap, LANES), jnp.float32)
        for g in range(kv_heads):
            columns = pl.ds(pl.multiple_of(first_column + g * HD, HD), HD)
            group_heads = [g * group + r for r in range(group)]
            query = jnp.concatenate(
                [q_buf[slot, :, h * HD:(h + 1) * HD] for h in group_heads], axis=0
            )
            peaks, sums = [], []
            for block in range(2 * blocks):
                k_ref, v_ref = caches[2 * (block // blocks):2 * (block // blocks) + 2]
                at = slice(block % blocks * KB, (block % blocks + 1) * KB)
                scores = lax.dot_general(
                    k_ref[slot, at, columns], query, (((1,), (1,)), ((), ())),
                    preferred_element_type=jnp.float32,
                )
                peak = jnp.max(scores, axis=0, keepdims=True)
                weights = jnp.exp2((scores - peak) * TO_LOG2).astype(jnp.bfloat16)
                values = jnp.concatenate([v_ref[slot, at, columns], ones], axis=1)
                sums.append(
                    lax.dot_general(
                        weights, values, (((0,), (0,)), ((), ())),
                        preferred_element_type=jnp.float32,
                    )
                )
                peaks.append(peak * TO_LOG2)
            top = functools.reduce(jnp.maximum, peaks)
            factors = [top] + [jnp.exp2(peak - top) for peak in peaks]
            factors.append(jnp.zeros((SUBLANES - len(factors), packed), jnp.float32))
            factors = jnp.transpose(jnp.concatenate(factors, axis=0))
            total = sum(part * factors[:, i + 1:i + 2] for i, part in enumerate(sums))
            average = total[:, :HD] / total[:, HD:]
            log_total = factors[:, :1] + jnp.log2(total[:, HD:])
            for r, h in enumerate(group_heads):
                at = slice(r * cap, (r + 1) * cap)
                y_buf[slot, :, h * HD:(h + 1) * HD] = average[at]
                level = jnp.where(cap_lane == h, log_total[at], level)
        levels.append(level)

    level_of = []
    for slot in range(local_shards):
        level = dot(backs[slot], jnp.concatenate(parts_of(levels[slot], 3), axis=0))
        level_of.append(jnp.where(hits[slot], level, NEG_FILL))
    top = functools.reduce(jnp.maximum, level_of)
    shares = [
        jnp.where(hit, jnp.exp2(level - top), 0.0) for hit, level in zip(hits, level_of)
    ]
    share_sum = sum(shares)
    some = share_sum > 0.0
    share_sum = jnp.where(some, share_sum, 1.0)
    merged_level = jnp.where(some, top + jnp.log2(share_sum), NEG_FILL)
    scaled = []
    for slot in range(local_shards):
        share = sum(dot(picks[slot], part) for part in parts_of(shares[slot] / share_sum, 2))
        columns = [
            y_buf[slot, :, h * HD:(h + 1) * HD] * share[:, h:h + 1] for h in range(heads)
        ]
        scaled += parts_of(jnp.concatenate(columns, axis=1), 2)
    back_at = lane_iota((rows, 2 * local_shards * cap))
    back_place = lax.rem(back_at, cap).astype(jnp.float32)
    back_slot = lax.div(back_at, 2 * cap)
    back = functools.reduce(
        jnp.logical_or,
        [
            (back_slot == slot) & (back_place == place[:, slot:slot + 1]) & hits[slot]
            for slot in range(local_shards)
        ],
    )
    merged = dot(one_hot(back), jnp.concatenate(scaled, axis=0))
    stats = jnp.zeros((rows, LANES), jnp.float32)
    level_parts = parts_of(jnp.where(lane < heads, merged_level, 0.0), 3)
    for i, part in enumerate(level_parts):
        part = part.astype(jnp.float32)
        stats = stats + (pltpu.roll(part, PART * i, 1) if i else part)
    out = jnp.concatenate([merged, stats], axis=1).astype(jnp.bfloat16)
    out_ref[...] = out.reshape(out_ref.shape)


def attend(message, caches):
    devices, own_rows, columns = message.shape
    keys = caches[0]
    local_shards = keys.shape[0]
    cap = devices * own_rows // 2
    width = columns - LANES
    scores = 2 * cap * width // HD * local_shards * keys.shape[1]
    return pl.pallas_call(
        attend_body,
        out_shape=jax.ShapeDtypeStruct(message.shape, jnp.bfloat16),
        scratch_shapes=[
            pltpu.VMEM((local_shards, cap, width), jnp.bfloat16),
            pltpu.VMEM((local_shards, cap, width), jnp.float32),
        ],
        compiler_params=params(),
        cost_estimate=pl.CostEstimate(
            flops=4 * scores * HD, bytes_accessed=4 * keys.size, transcendentals=scores
        ),
        name="attend",
    )(message, *caches)


def finish_body(x_ref, out_ref):
    devices, own_rows, message = x_ref.shape
    width = message - LANES
    rows = devices * own_rows
    period = 2 * own_rows

    def over_chips(x, combine):
        x = functools.reduce(combine, [x[i] for i in range(x.shape[0])])
        shift = period
        while shift < SUBLANES:
            x = combine(x, pltpu.roll(x, shift, 0))
            shift *= 2
        return x

    def tiles(x):
        return x.reshape(rows // SUBLANES, SUBLANES, x.shape[1])

    x = x_ref[...].reshape(rows, message).astype(jnp.float32)
    stats = x[:, width:]
    level = stats
    for i in (1, 2):
        level = level + pltpu.roll(stats, LANES - PART * i, 1)
    level = tiles(level)
    factor = jnp.exp2(level - over_chips(level, jnp.maximum)[None])
    share = factor / over_chips(factor, jnp.add)[None]
    pieces = [
        over_chips(tiles(x[:, h * HD:(h + 1) * HD]) * share[:, :, h:h + 1], jnp.add)
        for h in range(width // HD)
    ]
    merged = jnp.concatenate(pieces, axis=1)
    out_ref[...] = jnp.concatenate(
        [merged[core * own_rows:(core + 1) * own_rows] for core in range(2)], axis=1
    ).astype(jnp.bfloat16)


def finish(received, own_rows, width):
    return pl.pallas_call(
        finish_body,
        out_shape=jax.ShapeDtypeStruct((own_rows, width), jnp.bfloat16),
        compiler_params=params(),
        name="finish",
    )(received)


def shards(devices, queries, cached_keys, cached_values, shard_hits):
    axes = ("shard", "seq")
    siblings = [(i, i ^ 1) for i in range(devices)]
    caches = (
        cached_keys,
        cached_values,
        lax.ppermute(cached_keys, axes, siblings),
        lax.ppermute(cached_values, axes, siblings),
    )
    message = pack(queries, shard_hits, devices)
    received = lax.all_to_all(message, axes, 0, 0)
    partial = attend(received, caches)
    received = lax.all_to_all(partial, axes, 0, 0)
    return finish(received, *queries.shape)


def solution(mesh):
    both = P(("shard", "seq"), None)
    cache = P("shard", "seq", None)
    return jax.shard_map(
        functools.partial(shards, mesh.size),
        mesh=mesh,
        in_specs=(both, cache, cache, both),
        out_specs=both,
        check_vma=False,
    )
```

```python
import functools
import math

import jax
import jax.numpy as jnp
from jax import lax
from jax.experimental import pallas as pl
from jax.experimental.pallas import tpu as pltpu
from jax.sharding import PartitionSpec as P

HD = 128
KB = 512
LANES = 128
NEG_FILL = -1e30
TO_LOG2 = math.log2(math.e) / math.sqrt(HD)
PACK_COST = 20_000_000_000
VMEM_LIMIT = 24 * 1024 * 1024
PART = 32
SUBLANES = 8


def params():
    return pltpu.CompilerParams(vmem_limit_bytes=VMEM_LIMIT)


def lane_iota(shape):
    return lax.broadcasted_iota(jnp.int32, shape, len(shape) - 1)


def one_hot(condition):
    return jnp.where(condition, 1.0, 0.0).astype(jnp.bfloat16)


def dot(a, b):
    return jnp.dot(a, b, preferred_element_type=jnp.float32)


def parts_of(x, count):
    parts = []
    for _ in range(count):
        part = x.astype(jnp.bfloat16)
        parts.append(part)
        x = x - part.astype(jnp.float32)
    return parts


def pack_body(x_ref, out_ref):
    half = (x_ref.shape[1] - LANES) // 2
    x = x_ref[...]
    for core in range(2):
        message = jnp.concatenate([x[:, core * half:(core + 1) * half], x[:, 2 * half:]], axis=1)
        out_ref[:, core] = jnp.broadcast_to(message[None], (out_ref.shape[0],) + message.shape)


def pack(queries, hits, devices):
    own_rows, width = queries.shape
    listed = jnp.pad(hits, ((0, 0), (width, LANES - hits.shape[1]))) > 0
    joined = jnp.where(listed, 1.0, jnp.pad(queries, ((0, 0), (0, LANES)))).astype(queries.dtype)
    shape = (devices // 2, 2, own_rows, width // 2 + LANES)
    out = pl.pallas_call(
        pack_body,
        out_shape=jax.ShapeDtypeStruct(shape, jnp.bfloat16),
        compiler_params=params(),
        cost_estimate=pl.CostEstimate(flops=PACK_COST, bytes_accessed=0, transcendentals=0),
        name="pack_queries",
    )(joined)
    return out.reshape(devices, own_rows, width // 2 + LANES)


def attend_body(x_ref, *refs):
    *caches, out_ref, q_buf, y_buf = refs
    devices, own_rows, message = x_ref.shape
    width = message - LANES
    heads = width // HD
    local_shards, positions, cache_width = caches[0].shape
    kv_heads = cache_width // HD // 2
    group = heads // kv_heads
    blocks = positions // KB
    rows = devices * own_rows
    cap = rows // 2
    packed = group * cap
    first_column = lax.rem(lax.axis_index("seq"), 2) * (kv_heads * HD)

    x = x_ref[...].reshape(rows, message)
    listed = x[:, width:].astype(jnp.float32)
    first = lax.axis_index("shard") * local_shards
    lane = lane_iota((rows, LANES))
    slots = jnp.zeros((rows, LANES), jnp.float32)
    for slot in range(local_shards):
        hit = jnp.sum(jnp.where(lane == first + slot, listed, 0.0), axis=1, keepdims=True)
        slots = jnp.where(lane == slot, hit, slots)
    hits = [slots[:, slot:slot + 1] > 0.0 for slot in range(local_shards)]
    row = lax.broadcasted_iota(jnp.int32, (rows, rows), 0)
    column = lax.broadcasted_iota(jnp.int32, (rows, rows), 1)
    place = dot(one_hot(column < row), slots.astype(jnp.bfloat16))
    slots_t = jnp.transpose(slots)[:SUBLANES]
    place_t = dot(slots_t.astype(jnp.bfloat16), one_hot(row < column))

    pick_at = lax.broadcasted_iota(jnp.int32, (cap, rows), 0).astype(jnp.float32)
    picks, backs = [], []
    for slot in range(local_shards):
        picks.append(
            one_hot((pick_at == place_t[slot:slot + 1]) & (slots_t[slot:slot + 1] > 0.0))
        )
        q_buf[slot] = dot(picks[slot], x[:, :width]).astype(jnp.bfloat16)
        back_at = lax.rem(lane_iota((rows, 3 * cap)), cap).astype(jnp.float32)
        backs.append(one_hot((back_at == place[:, slot:slot + 1]) & hits[slot]))

    mine = pl.ds(pl.multiple_of(first_column, HD), kv_heads * HD)
    caches = [ref.at[:, :, mine] for ref in caches]
    ones = jnp.ones((KB, LANES), jnp.bfloat16)
    cap_lane = lane_iota((cap, LANES))
    levels = []
    for slot in range(local_shards):
        level = jnp.zeros((cap, LANES), jnp.float32)
        for g in range(kv_heads):
            columns = slice(g * HD, (g + 1) * HD)
            group_heads = [g * group + r for r in range(group)]
            query = jnp.concatenate(
                [q_buf[slot, :, h * HD:(h + 1) * HD] for h in group_heads], axis=0
            )
            peaks, sums = [], []
            for block in range(2 * blocks):
                k_ref, v_ref = caches[2 * (block // blocks):2 * (block // blocks) + 2]
                at = slice(block % blocks * KB, (block % blocks + 1) * KB)
                scores = lax.dot_general(
                    k_ref[slot, at, columns], query, (((1,), (1,)), ((), ())),
                    preferred_element_type=jnp.float32,
                )
                peak = jnp.max(scores, axis=0, keepdims=True)
                weights = jnp.exp2((scores - peak) * TO_LOG2).astype(jnp.bfloat16)
                values = jnp.concatenate([v_ref[slot, at, columns], ones], axis=1)
                sums.append(
                    lax.dot_general(
                        weights, values, (((0,), (0,)), ((), ())),
                        preferred_element_type=jnp.float32,
                    )
                )
                peaks.append(peak * TO_LOG2)
            top = functools.reduce(jnp.maximum, peaks)
            factors = [top] + [jnp.exp2(peak - top) for peak in peaks]
            factors.append(jnp.zeros((SUBLANES - len(factors), packed), jnp.float32))
            factors = jnp.transpose(jnp.concatenate(factors, axis=0))
            total = sum(part * factors[:, i + 1:i + 2] for i, part in enumerate(sums))
            average = total[:, :HD] / total[:, HD:]
            log_total = factors[:, :1] + jnp.log2(total[:, HD:])
            for r, h in enumerate(group_heads):
                at = slice(r * cap, (r + 1) * cap)
                y_buf[slot, :, h * HD:(h + 1) * HD] = average[at]
                level = jnp.where(cap_lane == h, log_total[at], level)
        levels.append(level)

    level_of = []
    for slot in range(local_shards):
        level = dot(backs[slot], jnp.concatenate(parts_of(levels[slot], 3), axis=0))
        level_of.append(jnp.where(hits[slot], level, NEG_FILL))
    top = functools.reduce(jnp.maximum, level_of)
    shares = [
        jnp.where(hit, jnp.exp2(level - top), 0.0) for hit, level in zip(hits, level_of)
    ]
    share_sum = sum(shares)
    some = share_sum > 0.0
    share_sum = jnp.where(some, share_sum, 1.0)
    merged_level = jnp.where(some, top + jnp.log2(share_sum), NEG_FILL)
    scaled = []
    for slot in range(local_shards):
        share = sum(dot(picks[slot], part) for part in parts_of(shares[slot] / share_sum, 2))
        columns = [
            y_buf[slot, :, h * HD:(h + 1) * HD] * share[:, h:h + 1] for h in range(heads)
        ]
        scaled += parts_of(jnp.concatenate(columns, axis=1), 2)
    back_at = lane_iota((rows, 2 * local_shards * cap))
    back_place = lax.rem(back_at, cap).astype(jnp.float32)
    back_slot = lax.div(back_at, 2 * cap)
    back = functools.reduce(
        jnp.logical_or,
        [
            (back_slot == slot) & (back_place == place[:, slot:slot + 1]) & hits[slot]
            for slot in range(local_shards)
        ],
    )
    merged = dot(one_hot(back), jnp.concatenate(scaled, axis=0))
    stats = jnp.zeros((rows, LANES), jnp.float32)
    level_parts = parts_of(jnp.where(lane < heads, merged_level, 0.0), 3)
    for i, part in enumerate(level_parts):
        part = part.astype(jnp.float32)
        stats = stats + (pltpu.roll(part, PART * i, 1) if i else part)
    out = jnp.concatenate([merged, stats], axis=1).astype(jnp.bfloat16)
    out_ref[...] = out.reshape(out_ref.shape)


def attend(message, caches):
    devices, own_rows, columns = message.shape
    keys = caches[0]
    local_shards = keys.shape[0]
    cap = devices * own_rows // 2
    width = columns - LANES
    scores = 2 * cap * width // HD * local_shards * keys.shape[1]
    return pl.pallas_call(
        attend_body,
        out_shape=jax.ShapeDtypeStruct(message.shape, jnp.bfloat16),
        scratch_shapes=[
            pltpu.VMEM((local_shards, cap, width), jnp.bfloat16),
            pltpu.VMEM((local_shards, cap, width), jnp.float32),
        ],
        compiler_params=params(),
        cost_estimate=pl.CostEstimate(
            flops=4 * scores * HD, bytes_accessed=4 * keys.size, transcendentals=scores
        ),
        name="attend",
    )(message, *caches)


def finish_body(x_ref, out_ref):
    devices, own_rows, message = x_ref.shape
    width = message - LANES
    heads = width // HD
    rows = devices * own_rows
    period = 2 * own_rows

    def over_chips(x, combine):
        x = functools.reduce(combine, [x[i] for i in range(x.shape[0])])
        shift = period
        while shift < SUBLANES:
            x = combine(x, pltpu.roll(x, shift, 0))
            shift *= 2
        return x

    x = x_ref[...].reshape(rows, message)
    stats = x[:, width:].astype(jnp.float32)
    level = stats
    for i in (1, 2):
        level = level + pltpu.roll(stats, LANES - PART * i, 1)
    level = level.reshape(rows // SUBLANES, SUBLANES, LANES)
    factor = jnp.exp2(level - over_chips(level, jnp.maximum)[None])
    share = factor / over_chips(factor, jnp.add)[None]
    share = jnp.transpose(share.reshape(rows, LANES))[:heads]
    high, low = parts_of(share, 2)
    target = lax.broadcasted_iota(jnp.int32, (SUBLANES, rows), 0)
    source = lax.broadcasted_iota(jnp.int32, (SUBLANES, rows), 1)
    mine = target == lax.rem(source, period)
    high, low = high.astype(jnp.float32), low.astype(jnp.float32)
    pieces = []
    for h in range(heads):
        weights = jnp.concatenate(
            [jnp.where(mine, part[h:h + 1], 0.0) for part in (high, low)], axis=0
        ).astype(jnp.bfloat16)
        both = dot(weights, x[:, h * HD:(h + 1) * HD])
        pieces.append(both[:SUBLANES] + both[SUBLANES:])
    merged = jnp.concatenate(pieces, axis=1)
    out_ref[...] = jnp.concatenate(
        [merged[core * own_rows:(core + 1) * own_rows] for core in range(2)], axis=1
    ).astype(jnp.bfloat16)


def finish(received, own_rows, width):
    return pl.pallas_call(
        finish_body,
        out_shape=jax.ShapeDtypeStruct((own_rows, width), jnp.bfloat16),
        compiler_params=params(),
        name="finish",
    )(received)


def shards(devices, queries, cached_keys, cached_values, shard_hits):
    axes = ("shard", "seq")
    siblings = [(i, i ^ 1) for i in range(devices)]
    caches = (
        cached_keys,
        cached_values,
        lax.ppermute(cached_keys, axes, siblings),
        lax.ppermute(cached_values, axes, siblings),
    )
    message = pack(queries, shard_hits, devices)
    received = lax.all_to_all(message, axes, 0, 0)
    partial = attend(received, caches)
    received = lax.all_to_all(partial, axes, 0, 0)
    return finish(received, *queries.shape)


def solution(mesh):
    both = P(("shard", "seq"), None)
    cache = P("shard", "seq", None)
    return jax.shard_map(
        functools.partial(shards, mesh.size),
        mesh=mesh,
        in_specs=(both, cache, cache, both),
        out_specs=both,
        check_vma=False,
    )
```

```python
import functools
import math

import jax
import jax.numpy as jnp
from jax import lax
from jax.experimental import pallas as pl
from jax.experimental.pallas import tpu as pltpu
from jax.sharding import PartitionSpec as P

HD = 128
KB = 512
LANES = 128
NEG_FILL = -1e30
TO_LOG2 = math.log2(math.e) / math.sqrt(HD)
PACK_COST = 20_000_000_000
VMEM_LIMIT = 24 * 1024 * 1024
PART = 32
SUBLANES = 8


def params():
    return pltpu.CompilerParams(vmem_limit_bytes=VMEM_LIMIT)


def lane_iota(shape):
    return lax.broadcasted_iota(jnp.int32, shape, len(shape) - 1)


def one_hot(condition):
    return jnp.where(condition, 1.0, 0.0).astype(jnp.bfloat16)


def dot(a, b):
    return jnp.dot(a, b, preferred_element_type=jnp.float32)


def parts_of(x, count):
    parts = []
    for _ in range(count):
        part = x.astype(jnp.bfloat16)
        parts.append(part)
        x = x - part.astype(jnp.float32)
    return parts


def pack_body(x_ref, out_ref):
    half = (x_ref.shape[1] - LANES) // 2
    x = x_ref[...]
    for core in range(2):
        message = jnp.concatenate([x[:, core * half:(core + 1) * half], x[:, 2 * half:]], axis=1)
        out_ref[:, core] = jnp.broadcast_to(message[None], (out_ref.shape[0],) + message.shape)


def pack(queries, hits, devices):
    own_rows, width = queries.shape
    listed = jnp.pad(hits, ((0, 0), (width, LANES - hits.shape[1]))) > 0
    joined = jnp.where(listed, 1.0, jnp.pad(queries, ((0, 0), (0, LANES)))).astype(queries.dtype)
    shape = (devices // 2, 2, own_rows, width // 2 + LANES)
    out = pl.pallas_call(
        pack_body,
        out_shape=jax.ShapeDtypeStruct(shape, jnp.bfloat16),
        compiler_params=params(),
        cost_estimate=pl.CostEstimate(flops=PACK_COST, bytes_accessed=0, transcendentals=0),
        name="pack_queries",
    )(joined)
    return out.reshape(devices, own_rows, width // 2 + LANES)


def attend_body(x_ref, *refs):
    *caches, out_ref, q_buf, y_buf = refs
    devices, own_rows, message = x_ref.shape
    width = message - LANES
    heads = width // HD
    local_shards, positions, cache_width = caches[0].shape
    kv_heads = cache_width // HD // 2
    group = heads // kv_heads
    blocks = positions // KB
    rows = devices * own_rows
    cap = rows // 2
    packed = group * cap
    first_column = lax.rem(lax.axis_index("seq"), 2) * (kv_heads * HD)

    x = x_ref[...].reshape(rows, message)
    listed = x[:, width:].astype(jnp.float32)
    first = lax.axis_index("shard") * local_shards
    lane = lane_iota((rows, LANES))
    slots = jnp.zeros((rows, LANES), jnp.float32)
    for slot in range(local_shards):
        hit = jnp.sum(jnp.where(lane == first + slot, listed, 0.0), axis=1, keepdims=True)
        slots = jnp.where(lane == slot, hit, slots)
    hits = [slots[:, slot:slot + 1] > 0.0 for slot in range(local_shards)]
    row = lax.broadcasted_iota(jnp.int32, (rows, rows), 0)
    column = lax.broadcasted_iota(jnp.int32, (rows, rows), 1)
    place = dot(one_hot(column < row), slots.astype(jnp.bfloat16))
    slots_t = jnp.transpose(slots)[:SUBLANES]
    place_t = dot(slots_t.astype(jnp.bfloat16), one_hot(row < column))

    pick_at = lax.broadcasted_iota(jnp.int32, (cap, rows), 0).astype(jnp.float32)
    picks, backs = [], []
    for slot in range(local_shards):
        picks.append(
            one_hot((pick_at == place_t[slot:slot + 1]) & (slots_t[slot:slot + 1] > 0.0))
        )
        q_buf[slot] = dot(picks[slot], x[:, :width]).astype(jnp.bfloat16)
        back_at = lax.rem(lane_iota((rows, 3 * cap)), cap).astype(jnp.float32)
        backs.append(one_hot((back_at == place[:, slot:slot + 1]) & hits[slot]))

    mine = pl.ds(pl.multiple_of(first_column, HD), kv_heads * HD)
    caches = [ref.at[:, :, mine] for ref in caches]
    ones = jnp.ones((KB, LANES), jnp.bfloat16)
    cap_lane = lane_iota((cap, LANES))
    levels = [jnp.zeros((cap, LANES), jnp.float32) for _ in range(local_shards)]
    for g in range(kv_heads):
        for slot in range(local_shards):
            level = levels[slot]
            columns = slice(g * HD, (g + 1) * HD)
            group_heads = [g * group + r for r in range(group)]
            query = jnp.concatenate(
                [q_buf[slot, :, h * HD:(h + 1) * HD] for h in group_heads], axis=0
            )
            peaks, sums = [], []
            for block in range(2 * blocks):
                k_ref, v_ref = caches[2 * (block // blocks):2 * (block // blocks) + 2]
                at = slice(block % blocks * KB, (block % blocks + 1) * KB)
                scores = lax.dot_general(
                    k_ref[slot, at, columns], query, (((1,), (1,)), ((), ())),
                    preferred_element_type=jnp.float32,
                )
                peak = jnp.max(scores, axis=0, keepdims=True)
                weights = jnp.exp2((scores - peak) * TO_LOG2).astype(jnp.bfloat16)
                values = jnp.concatenate([v_ref[slot, at, columns], ones], axis=1)
                sums.append(
                    lax.dot_general(
                        weights, values, (((0,), (0,)), ((), ())),
                        preferred_element_type=jnp.float32,
                    )
                )
                peaks.append(peak * TO_LOG2)
            top = functools.reduce(jnp.maximum, peaks)
            factors = [top] + [jnp.exp2(peak - top) for peak in peaks]
            factors.append(jnp.zeros((SUBLANES - len(factors), packed), jnp.float32))
            factors = jnp.transpose(jnp.concatenate(factors, axis=0))
            total = sum(part * factors[:, i + 1:i + 2] for i, part in enumerate(sums))
            average = total[:, :HD] * pl.reciprocal(total[:, HD:])
            log_total = factors[:, :1] + jnp.log2(total[:, HD:])
            for r, h in enumerate(group_heads):
                at = slice(r * cap, (r + 1) * cap)
                y_buf[slot, :, h * HD:(h + 1) * HD] = average[at]
                level = jnp.where(cap_lane == h, log_total[at], level)
            levels[slot] = level

    level_of = []
    for slot in range(local_shards):
        level = dot(backs[slot], jnp.concatenate(parts_of(levels[slot], 3), axis=0))
        level_of.append(jnp.where(hits[slot], level, NEG_FILL))
    top = functools.reduce(jnp.maximum, level_of)
    shares = [
        jnp.where(hit, jnp.exp2(level - top), 0.0) for hit, level in zip(hits, level_of)
    ]
    share_sum = sum(shares)
    some = share_sum > 0.0
    share_sum = jnp.where(some, share_sum, 1.0)
    merged_level = jnp.where(some, top + jnp.log2(share_sum), NEG_FILL)
    scaled = []
    for slot in range(local_shards):
        share = sum(dot(picks[slot], part) for part in parts_of(shares[slot] / share_sum, 2))
        columns = [
            y_buf[slot, :, h * HD:(h + 1) * HD] * share[:, h:h + 1] for h in range(heads)
        ]
        scaled += parts_of(jnp.concatenate(columns, axis=1), 2)
    back_at = lane_iota((rows, 2 * local_shards * cap))
    back_place = lax.rem(back_at, cap).astype(jnp.float32)
    back_slot = lax.div(back_at, 2 * cap)
    back = functools.reduce(
        jnp.logical_or,
        [
            (back_slot == slot) & (back_place == place[:, slot:slot + 1]) & hits[slot]
            for slot in range(local_shards)
        ],
    )
    merged = dot(one_hot(back), jnp.concatenate(scaled, axis=0))
    stats = jnp.zeros((rows, LANES), jnp.float32)
    level_parts = parts_of(jnp.where(lane < heads, merged_level, 0.0), 3)
    for i, part in enumerate(level_parts):
        part = part.astype(jnp.float32)
        stats = stats + (pltpu.roll(part, PART * i, 1) if i else part)
    out = jnp.concatenate([merged, stats], axis=1).astype(jnp.bfloat16)
    out_ref[...] = out.reshape(out_ref.shape)


def attend(message, caches):
    devices, own_rows, columns = message.shape
    keys = caches[0]
    local_shards = keys.shape[0]
    cap = devices * own_rows // 2
    width = columns - LANES
    scores = 2 * cap * width // HD * local_shards * keys.shape[1]
    return pl.pallas_call(
        attend_body,
        out_shape=jax.ShapeDtypeStruct(message.shape, jnp.bfloat16),
        scratch_shapes=[
            pltpu.VMEM((local_shards, cap, width), jnp.bfloat16),
            pltpu.VMEM((local_shards, cap, width), jnp.float32),
        ],
        compiler_params=params(),
        cost_estimate=pl.CostEstimate(
            flops=4 * scores * HD, bytes_accessed=4 * keys.size, transcendentals=scores
        ),
        name="attend",
    )(message, *caches)


def finish_body(x_ref, out_ref):
    devices, own_rows, message = x_ref.shape
    width = message - LANES
    heads = width // HD
    rows = devices * own_rows
    period = 2 * own_rows

    def over_chips(x, combine):
        x = functools.reduce(combine, [x[i] for i in range(x.shape[0])])
        shift = period
        while shift < SUBLANES:
            x = combine(x, pltpu.roll(x, shift, 0))
            shift *= 2
        return x

    x = x_ref[...].reshape(rows, message)
    stats = x[:, width:].astype(jnp.float32)
    level = stats
    for i in (1, 2):
        level = level + pltpu.roll(stats, LANES - PART * i, 1)
    level = level.reshape(rows // SUBLANES, SUBLANES, LANES)
    factor = jnp.exp2(level - over_chips(level, jnp.maximum)[None])
    share = factor / over_chips(factor, jnp.add)[None]
    share = jnp.transpose(share.reshape(rows, LANES))[:heads]
    high, low = parts_of(share, 2)
    target = lax.broadcasted_iota(jnp.int32, (SUBLANES, rows), 0)
    source = lax.broadcasted_iota(jnp.int32, (SUBLANES, rows), 1)
    mine = target == lax.rem(source, period)
    high, low = high.astype(jnp.float32), low.astype(jnp.float32)
    pieces = []
    for h in range(heads):
        weights = jnp.concatenate(
            [jnp.where(mine, part[h:h + 1], 0.0) for part in (high, low)], axis=0
        ).astype(jnp.bfloat16)
        both = dot(weights, x[:, h * HD:(h + 1) * HD])
        pieces.append(both[:SUBLANES] + both[SUBLANES:])
    merged = jnp.concatenate(pieces, axis=1)
    out_ref[...] = jnp.concatenate(
        [merged[core * own_rows:(core + 1) * own_rows] for core in range(2)], axis=1
    ).astype(jnp.bfloat16)


def finish(received, own_rows, width):
    return pl.pallas_call(
        finish_body,
        out_shape=jax.ShapeDtypeStruct((own_rows, width), jnp.bfloat16),
        compiler_params=params(),
        name="finish",
    )(received)


def shards(devices, queries, cached_keys, cached_values, shard_hits):
    axes = ("shard", "seq")
    siblings = [(i, i ^ 1) for i in range(devices)]
    caches = (
        cached_keys,
        cached_values,
        lax.ppermute(cached_keys, axes, siblings),
        lax.ppermute(cached_values, axes, siblings),
    )
    message = pack(queries, shard_hits, devices)
    received = lax.all_to_all(message, axes, 0, 0)
    partial = attend(received, caches)
    received = lax.all_to_all(partial, axes, 0, 0)
    return finish(received, *queries.shape)


def solution(mesh):
    both = P(("shard", "seq"), None)
    cache = P("shard", "seq", None)
    return jax.shard_map(
        functools.partial(shards, mesh.size),
        mesh=mesh,
        in_specs=(both, cache, cache, both),
        out_specs=both,
        check_vma=False,
    )
```

```python
import functools
import math

import jax
import jax.numpy as jnp
from jax import lax
from jax.experimental import pallas as pl
from jax.experimental.pallas import tpu as pltpu
from jax.sharding import PartitionSpec as P

HD = 128
KB = 512
LANES = 128
NEG_FILL = -1e30
TO_LOG2 = math.log2(math.e) / math.sqrt(HD)
PACK_COST = 20_000_000_000
VMEM_LIMIT = 24 * 1024 * 1024
PART = 32
SUBLANES = 8


def params():
    return pltpu.CompilerParams(vmem_limit_bytes=VMEM_LIMIT)


def lane_iota(shape):
    return lax.broadcasted_iota(jnp.int32, shape, len(shape) - 1)


def one_hot(condition):
    return jnp.where(condition, 1.0, 0.0).astype(jnp.bfloat16)


def dot(a, b):
    return jnp.dot(a, b, preferred_element_type=jnp.float32)


def parts_of(x, count):
    parts = []
    for _ in range(count):
        part = x.astype(jnp.bfloat16)
        parts.append(part)
        x = x - part.astype(jnp.float32)
    return parts


def pack_body(x_ref, out_ref):
    half = (x_ref.shape[1] - LANES) // 2
    x = x_ref[...]
    for core in range(2):
        message = jnp.concatenate([x[:, core * half:(core + 1) * half], x[:, 2 * half:]], axis=1)
        out_ref[:, core] = jnp.broadcast_to(message[None], (out_ref.shape[0],) + message.shape)


def pack(queries, hits, devices):
    own_rows, width = queries.shape
    listed = jnp.pad(hits, ((0, 0), (width, LANES - hits.shape[1]))) > 0
    joined = jnp.where(listed, 1.0, jnp.pad(queries, ((0, 0), (0, LANES)))).astype(queries.dtype)
    shape = (devices // 2, 2, own_rows, width // 2 + LANES)
    out = pl.pallas_call(
        pack_body,
        out_shape=jax.ShapeDtypeStruct(shape, jnp.bfloat16),
        compiler_params=params(),
        cost_estimate=pl.CostEstimate(flops=PACK_COST, bytes_accessed=0, transcendentals=0),
        name="pack_queries",
    )(joined)
    return out.reshape(devices, own_rows, width // 2 + LANES)


def attend_body(x_ref, *refs):
    *caches, out_ref, q_buf, y_buf = refs
    devices, own_rows, message = x_ref.shape
    width = message - LANES
    heads = width // HD
    local_shards, positions, cache_width = caches[0].shape
    kv_heads = cache_width // HD // 2
    group = heads // kv_heads
    blocks = positions // KB
    rows = devices * own_rows
    cap = rows // 2
    packed = group * cap
    first_column = lax.rem(lax.axis_index("seq"), 2) * (kv_heads * HD)

    x = x_ref[...].reshape(rows, message)
    listed = x[:, width:].astype(jnp.float32)
    first = lax.axis_index("shard") * local_shards
    lane = lane_iota((rows, LANES))
    slots = pltpu.roll(listed, lax.rem(LANES - first, LANES), 1)
    hits = [slots[:, slot:slot + 1] > 0.0 for slot in range(local_shards)]
    row = lax.broadcasted_iota(jnp.int32, (rows, rows), 0)
    column = lax.broadcasted_iota(jnp.int32, (rows, rows), 1)
    place = dot(one_hot(column < row), slots.astype(jnp.bfloat16))
    slots_t = jnp.transpose(slots)[:SUBLANES]
    place_t = dot(slots_t.astype(jnp.bfloat16), one_hot(row < column))

    pick_at = lax.broadcasted_iota(jnp.int32, (cap, rows), 0).astype(jnp.float32)
    picks, backs = [], []
    for slot in range(local_shards):
        picks.append(
            one_hot((pick_at == place_t[slot:slot + 1]) & (slots_t[slot:slot + 1] > 0.0))
        )
        q_buf[slot] = dot(picks[slot], x[:, :width]).astype(jnp.bfloat16)
        back_at = lax.rem(lane_iota((rows, 3 * cap)), cap).astype(jnp.float32)
        backs.append(one_hot((back_at == place[:, slot:slot + 1]) & hits[slot]))

    mine = pl.ds(pl.multiple_of(first_column, HD), kv_heads * HD)
    caches = [ref.at[:, :, mine] for ref in caches]
    ones = jnp.ones((KB, LANES), jnp.bfloat16)
    cap_lane = lane_iota((cap, LANES))
    levels = [jnp.zeros((cap, LANES), jnp.float32) for _ in range(local_shards)]
    for g in range(kv_heads):
        for slot in range(local_shards):
            level = levels[slot]
            columns = slice(g * HD, (g + 1) * HD)
            group_heads = [g * group + r for r in range(group)]
            query = jnp.concatenate(
                [q_buf[slot, :, h * HD:(h + 1) * HD] for h in group_heads], axis=0
            )
            peaks, sums = [], []
            for block in range(2 * blocks):
                k_ref, v_ref = caches[2 * (block // blocks):2 * (block // blocks) + 2]
                at = slice(block % blocks * KB, (block % blocks + 1) * KB)
                scores = lax.dot_general(
                    k_ref[slot, at, columns], query, (((1,), (1,)), ((), ())),
                    preferred_element_type=jnp.float32,
                )
                peak = jnp.max(scores, axis=0, keepdims=True)
                weights = jnp.exp2((scores - peak) * TO_LOG2).astype(jnp.bfloat16)
                values = jnp.concatenate([v_ref[slot, at, columns], ones], axis=1)
                sums.append(
                    lax.dot_general(
                        weights, values, (((0,), (0,)), ((), ())),
                        preferred_element_type=jnp.float32,
                    )
                )
                peaks.append(peak * TO_LOG2)
            top = functools.reduce(jnp.maximum, peaks)
            factors = [top] + [jnp.exp2(peak - top) for peak in peaks]
            factors.append(jnp.zeros((SUBLANES - len(factors), packed), jnp.float32))
            factors = jnp.transpose(jnp.concatenate(factors, axis=0))
            spread = [
                jnp.broadcast_to(factors[:, i + 1:i + 2], (packed, HD)) for i in range(len(sums))
            ]
            total = sum(
                part * jnp.concatenate([factor] * 2, axis=1) for part, factor in zip(sums, spread)
            )
            average = total[:, :HD] * pl.reciprocal(total[:, HD:])
            log_total = factors[:, :1] + jnp.log2(total[:, HD:])
            for r, h in enumerate(group_heads):
                at = slice(r * cap, (r + 1) * cap)
                y_buf[slot, :, h * HD:(h + 1) * HD] = average[at]
                level = jnp.where(cap_lane == h, log_total[at], level)
            levels[slot] = level

    level_of = []
    for slot in range(local_shards):
        level = dot(backs[slot], jnp.concatenate(parts_of(levels[slot], 3), axis=0))
        level_of.append(jnp.where(hits[slot], level, NEG_FILL))
    top = functools.reduce(jnp.maximum, level_of)
    shares = [
        jnp.where(hit, jnp.exp2(level - top), 0.0) for hit, level in zip(hits, level_of)
    ]
    share_sum = sum(shares)
    some = share_sum > 0.0
    share_sum = jnp.where(some, share_sum, 1.0)
    merged_level = jnp.where(some, top + jnp.log2(share_sum), NEG_FILL)
    scaled = []
    for slot in range(local_shards):
        share = sum(dot(picks[slot], part) for part in parts_of(shares[slot] / share_sum, 2))
        columns = [
            y_buf[slot, :, h * HD:(h + 1) * HD] * share[:, h:h + 1] for h in range(heads)
        ]
        scaled += parts_of(jnp.concatenate(columns, axis=1), 2)
    back_at = lane_iota((rows, 2 * local_shards * cap))
    back_place = lax.rem(back_at, cap).astype(jnp.float32)
    back_slot = lax.div(back_at, 2 * cap)
    back = functools.reduce(
        jnp.logical_or,
        [
            (back_slot == slot) & (back_place == place[:, slot:slot + 1]) & hits[slot]
            for slot in range(local_shards)
        ],
    )
    merged = dot(one_hot(back), jnp.concatenate(scaled, axis=0))
    stats = jnp.zeros((rows, LANES), jnp.float32)
    level_parts = parts_of(jnp.where(lane < heads, merged_level, 0.0), 3)
    for i, part in enumerate(level_parts):
        part = part.astype(jnp.float32)
        stats = stats + (pltpu.roll(part, PART * i, 1) if i else part)
    out = jnp.concatenate([merged, stats], axis=1).astype(jnp.bfloat16)
    out_ref[...] = out.reshape(out_ref.shape)


def attend(message, caches):
    devices, own_rows, columns = message.shape
    keys = caches[0]
    local_shards = keys.shape[0]
    cap = devices * own_rows // 2
    width = columns - LANES
    scores = 2 * cap * width // HD * local_shards * keys.shape[1]
    return pl.pallas_call(
        attend_body,
        out_shape=jax.ShapeDtypeStruct(message.shape, jnp.bfloat16),
        scratch_shapes=[
            pltpu.VMEM((local_shards, cap, width), jnp.bfloat16),
            pltpu.VMEM((local_shards, cap, width), jnp.float32),
        ],
        compiler_params=params(),
        cost_estimate=pl.CostEstimate(
            flops=4 * scores * HD, bytes_accessed=4 * keys.size, transcendentals=scores
        ),
        name="attend",
    )(message, *caches)


def finish_body(x_ref, out_ref):
    devices, own_rows, message = x_ref.shape
    width = message - LANES
    heads = width // HD
    rows = devices * own_rows
    period = 2 * own_rows

    def over_chips(x, combine):
        x = functools.reduce(combine, [x[i] for i in range(x.shape[0])])
        shift = period
        while shift < SUBLANES:
            x = combine(x, pltpu.roll(x, shift, 0))
            shift *= 2
        return x

    x = x_ref[...].reshape(rows, message)
    stats = x[:, width:].astype(jnp.float32)
    top = over_chips(stats.reshape(rows // SUBLANES, SUBLANES, LANES), jnp.maximum)[None]
    level = stats
    for i in (1, 2):
        level = level + pltpu.roll(stats, LANES - PART * i, 1)
    level = level.reshape(rows // SUBLANES, SUBLANES, LANES)
    factor = jnp.where(lane_iota(level.shape) < heads, jnp.exp2(level - top), 0.0)
    total = over_chips(factor, jnp.add)[None]
    share = factor * pl.reciprocal(jnp.where(total > 0.0, total, 1.0))
    share = jnp.transpose(share.reshape(rows, LANES))[:heads]
    high, low = parts_of(share, 2)
    target = lax.broadcasted_iota(jnp.int32, (SUBLANES, rows), 0)
    source = lax.broadcasted_iota(jnp.int32, (SUBLANES, rows), 1)
    mine = target == lax.rem(source, period)
    high, low = high.astype(jnp.float32), low.astype(jnp.float32)
    pieces = []
    for h in range(heads):
        weights = jnp.concatenate(
            [jnp.where(mine, part[h:h + 1], 0.0) for part in (high, low)], axis=0
        ).astype(jnp.bfloat16)
        both = dot(weights, x[:, h * HD:(h + 1) * HD])
        pieces.append(both[:SUBLANES] + both[SUBLANES:])
    merged = jnp.concatenate(pieces, axis=1)
    out_ref[...] = jnp.concatenate(
        [merged[core * own_rows:(core + 1) * own_rows] for core in range(2)], axis=1
    ).astype(jnp.bfloat16)


def finish(received, own_rows, width):
    return pl.pallas_call(
        finish_body,
        out_shape=jax.ShapeDtypeStruct((own_rows, width), jnp.bfloat16),
        compiler_params=params(),
        name="finish",
    )(received)


def shards(devices, queries, cached_keys, cached_values, shard_hits):
    axes = ("shard", "seq")
    siblings = [(i, i ^ 1) for i in range(devices)]
    caches = (
        cached_keys,
        cached_values,
        lax.ppermute(cached_keys, axes, siblings),
        lax.ppermute(cached_values, axes, siblings),
    )
    message = pack(queries, shard_hits, devices)
    received = lax.all_to_all(message, axes, 0, 0)
    partial = attend(received, caches)
    received = lax.all_to_all(partial, axes, 0, 0)
    return finish(received, *queries.shape)


def solution(mesh):
    both = P(("shard", "seq"), None)
    cache = P("shard", "seq", None)
    return jax.shard_map(
        functools.partial(shards, mesh.size),
        mesh=mesh,
        in_specs=(both, cache, cache, both),
        out_specs=both,
        check_vma=False,
    )
```

```python
import functools
import math

import jax
import jax.numpy as jnp
from jax import lax
from jax.experimental import pallas as pl
from jax.experimental.pallas import tpu as pltpu
from jax.sharding import PartitionSpec as P

HD = 128
KB = 512
LANES = 128
NEG_FILL = -1e30
TO_LOG2 = math.log2(math.e) / math.sqrt(HD)
PACK_COST = 20_000_000_000
VMEM_LIMIT = 24 * 1024 * 1024
PART = 32
SUBLANES = 8


def params():
    return pltpu.CompilerParams(vmem_limit_bytes=VMEM_LIMIT)


def lane_iota(shape):
    return lax.broadcasted_iota(jnp.int32, shape, len(shape) - 1)


def one_hot(condition):
    return jnp.where(condition, 1.0, 0.0).astype(jnp.bfloat16)


def dot(a, b):
    return jnp.dot(a, b, preferred_element_type=jnp.float32)


def parts_of(x, count):
    parts = []
    for _ in range(count):
        part = x.astype(jnp.bfloat16)
        parts.append(part)
        x = x - part.astype(jnp.float32)
    return parts


def pack_body(x_ref, out_ref):
    half = (x_ref.shape[1] - LANES) // 2
    x = x_ref[...]
    for core in range(2):
        message = jnp.concatenate([x[:, core * half:(core + 1) * half], x[:, 2 * half:]], axis=1)
        out_ref[:, core] = jnp.broadcast_to(message[None], (out_ref.shape[0],) + message.shape)


def pack(queries, hits, devices):
    own_rows, width = queries.shape
    listed = jnp.pad(hits, ((0, 0), (width, LANES - hits.shape[1]))) > 0
    joined = jnp.where(listed, 1.0, jnp.pad(queries, ((0, 0), (0, LANES)))).astype(queries.dtype)
    shape = (devices // 2, 2, own_rows, width // 2 + LANES)
    out = pl.pallas_call(
        pack_body,
        out_shape=jax.ShapeDtypeStruct(shape, jnp.bfloat16),
        compiler_params=params(),
        cost_estimate=pl.CostEstimate(flops=PACK_COST, bytes_accessed=0, transcendentals=0),
        name="pack_queries",
    )(joined)
    return out.reshape(devices, own_rows, width // 2 + LANES)


def attend_body(x_ref, *refs):
    *caches, out_ref, q_buf, y_buf = refs
    devices, own_rows, message = x_ref.shape
    width = message - LANES
    heads = width // HD
    local_shards, positions, cache_width = caches[0].shape
    kv_heads = cache_width // HD // 2
    group = heads // kv_heads
    blocks = positions // KB
    rows = devices * own_rows
    cap = rows // 2
    packed = group * cap
    first_column = lax.rem(lax.axis_index("seq"), 2) * (kv_heads * HD)

    x = x_ref[...].reshape(rows, message)
    listed = x[:, width:].astype(jnp.float32)
    first = lax.axis_index("shard") * local_shards
    lane = lane_iota((rows, LANES))
    slots = pltpu.roll(listed, lax.rem(LANES - first, LANES), 1)
    hits = [slots[:, slot:slot + 1] > 0.0 for slot in range(local_shards)]
    row = lax.broadcasted_iota(jnp.int32, (rows, rows), 0)
    column = lax.broadcasted_iota(jnp.int32, (rows, rows), 1)
    place = dot(one_hot(column < row), slots.astype(jnp.bfloat16))
    slots_t = jnp.transpose(slots)[:SUBLANES]
    place_t = dot(slots_t.astype(jnp.bfloat16), one_hot(row < column))

    pick_at = lax.broadcasted_iota(jnp.int32, (cap, rows), 0).astype(jnp.float32)
    picks, backs = [], []
    for slot in range(local_shards):
        picks.append(
            one_hot((pick_at == place_t[slot:slot + 1]) & (slots_t[slot:slot + 1] > 0.0))
        )
        back_at = lax.rem(lane_iota((rows, 3 * cap)), cap).astype(jnp.float32)
        backs.append(one_hot((back_at == place[:, slot:slot + 1]) & hits[slot]))

    mine = pl.ds(pl.multiple_of(first_column, HD), kv_heads * HD)
    caches = [ref.at[:, :, mine] for ref in caches]
    picked = dot(jnp.concatenate(picks, axis=0), x[:, :width]).astype(jnp.bfloat16)
    for slot in range(local_shards):
        q_buf[slot] = picked[slot * cap:(slot + 1) * cap]
    ones = jnp.ones((KB, LANES), jnp.bfloat16)
    cap_lane = lane_iota((cap, LANES))
    levels = [jnp.zeros((cap, LANES), jnp.float32) for _ in range(local_shards)]
    for g in range(kv_heads):
        for slot in range(local_shards):
            level = levels[slot]
            columns = slice(g * HD, (g + 1) * HD)
            group_heads = [g * group + r for r in range(group)]
            query = jnp.concatenate(
                [q_buf[slot, :, h * HD:(h + 1) * HD] for h in group_heads], axis=0
            )
            peaks, sums = [], []
            for block in range(2 * blocks):
                k_ref, v_ref = caches[2 * (block // blocks):2 * (block // blocks) + 2]
                at = slice(block % blocks * KB, (block % blocks + 1) * KB)
                scores = lax.dot_general(
                    k_ref[slot, at, columns], query, (((1,), (1,)), ((), ())),
                    preferred_element_type=jnp.float32,
                )
                peak = jnp.max(scores, axis=0, keepdims=True)
                weights = jnp.exp2((scores - peak) * TO_LOG2).astype(jnp.bfloat16)
                values = jnp.concatenate([v_ref[slot, at, columns], ones], axis=1)
                sums.append(
                    lax.dot_general(
                        weights, values, (((0,), (0,)), ((), ())),
                        preferred_element_type=jnp.float32,
                    )
                )
                peaks.append(peak * TO_LOG2)
            top = functools.reduce(jnp.maximum, peaks)
            factors = [top] + [jnp.exp2(peak - top) for peak in peaks]
            factors.append(jnp.zeros((SUBLANES - len(factors), packed), jnp.float32))
            factors = jnp.transpose(jnp.concatenate(factors, axis=0))
            spread = [
                jnp.broadcast_to(factors[:, i + 1:i + 2], (packed, HD)) for i in range(len(sums))
            ]
            total = sum(
                part * jnp.concatenate([factor] * 2, axis=1) for part, factor in zip(sums, spread)
            )
            average = total[:, :HD] * pl.reciprocal(total[:, HD:])
            log_total = factors[:, :1] + jnp.log2(total[:, HD:])
            for r, h in enumerate(group_heads):
                at = slice(r * cap, (r + 1) * cap)
                y_buf[slot, :, h * HD:(h + 1) * HD] = average[at]
                level = jnp.where(cap_lane == h, log_total[at], level)
            levels[slot] = level

    level_of = []
    for slot in range(local_shards):
        level = dot(backs[slot], jnp.concatenate(parts_of(levels[slot], 3), axis=0))
        level_of.append(jnp.where(hits[slot], level, NEG_FILL))
    top = functools.reduce(jnp.maximum, level_of)
    shares = [
        jnp.where(hit, jnp.exp2(level - top), 0.0) for hit, level in zip(hits, level_of)
    ]
    share_sum = sum(shares)
    some = share_sum > 0.0
    share_sum = jnp.where(some, share_sum, 1.0)
    merged_level = jnp.where(some, top + jnp.log2(share_sum), NEG_FILL)
    scaled = []
    for slot in range(local_shards):
        share = sum(dot(picks[slot], part) for part in parts_of(shares[slot] / share_sum, 2))
        columns = [
            y_buf[slot, :, h * HD:(h + 1) * HD] * share[:, h:h + 1] for h in range(heads)
        ]
        scaled += parts_of(jnp.concatenate(columns, axis=1), 2)
    back_at = lane_iota((rows, 2 * local_shards * cap))
    back_place = lax.rem(back_at, cap).astype(jnp.float32)
    back_slot = lax.div(back_at, 2 * cap)
    back = functools.reduce(
        jnp.logical_or,
        [
            (back_slot == slot) & (back_place == place[:, slot:slot + 1]) & hits[slot]
            for slot in range(local_shards)
        ],
    )
    merged = dot(one_hot(back), jnp.concatenate(scaled, axis=0))
    stats = jnp.zeros((rows, LANES), jnp.float32)
    level_parts = parts_of(jnp.where(lane < heads, merged_level, 0.0), 3)
    for i, part in enumerate(level_parts):
        part = part.astype(jnp.float32)
        stats = stats + (pltpu.roll(part, PART * i, 1) if i else part)
    out = jnp.concatenate([merged, stats], axis=1).astype(jnp.bfloat16)
    out_ref[...] = out.reshape(out_ref.shape)


def attend(message, caches):
    devices, own_rows, columns = message.shape
    keys = caches[0]
    local_shards = keys.shape[0]
    cap = devices * own_rows // 2
    width = columns - LANES
    scores = 2 * cap * width // HD * local_shards * keys.shape[1]
    return pl.pallas_call(
        attend_body,
        out_shape=jax.ShapeDtypeStruct(message.shape, jnp.bfloat16),
        scratch_shapes=[
            pltpu.VMEM((local_shards, cap, width), jnp.bfloat16),
            pltpu.VMEM((local_shards, cap, width), jnp.float32),
        ],
        compiler_params=params(),
        cost_estimate=pl.CostEstimate(
            flops=4 * scores * HD, bytes_accessed=4 * keys.size, transcendentals=scores
        ),
        name="attend",
    )(message, *caches)


def finish_body(x_ref, out_ref):
    devices, own_rows, message = x_ref.shape
    width = message - LANES
    heads = width // HD
    rows = devices * own_rows
    period = 2 * own_rows

    def over_chips(x, combine):
        x = functools.reduce(combine, [x[i] for i in range(x.shape[0])])
        shift = period
        while shift < SUBLANES:
            x = combine(x, pltpu.roll(x, shift, 0))
            shift *= 2
        return x

    x = x_ref[...].reshape(rows, message)
    stats = x[:, width:].astype(jnp.float32)
    top = over_chips(stats.reshape(rows // SUBLANES, SUBLANES, LANES), jnp.maximum)[None]
    level = stats
    for i in (1, 2):
        level = level + pltpu.roll(stats, LANES - PART * i, 1)
    level = level.reshape(rows // SUBLANES, SUBLANES, LANES)
    factor = jnp.where(lane_iota(level.shape) < heads, jnp.exp2(level - top), 0.0)
    total = over_chips(factor, jnp.add)[None]
    share = factor * pl.reciprocal(jnp.where(total > 0.0, total, 1.0))
    share = jnp.transpose(share.reshape(rows, LANES))[:heads]
    high, low = parts_of(share, 2)
    target = lax.broadcasted_iota(jnp.int32, (SUBLANES, rows), 0)
    source = lax.broadcasted_iota(jnp.int32, (SUBLANES, rows), 1)
    mine = target == lax.rem(source, period)
    high, low = high.astype(jnp.float32), low.astype(jnp.float32)
    pieces = []
    for h in range(heads):
        weights = jnp.concatenate(
            [jnp.where(mine, part[h:h + 1], 0.0) for part in (high, low)], axis=0
        ).astype(jnp.bfloat16)
        both = dot(weights, x[:, h * HD:(h + 1) * HD])
        pieces.append(both[:SUBLANES] + both[SUBLANES:])
    merged = jnp.concatenate(pieces, axis=1)
    out_ref[...] = jnp.concatenate(
        [merged[core * own_rows:(core + 1) * own_rows] for core in range(2)], axis=1
    ).astype(jnp.bfloat16)


def finish(received, own_rows, width):
    return pl.pallas_call(
        finish_body,
        out_shape=jax.ShapeDtypeStruct((own_rows, width), jnp.bfloat16),
        compiler_params=params(),
        name="finish",
    )(received)


def shards(devices, queries, cached_keys, cached_values, shard_hits):
    axes = ("shard", "seq")
    siblings = [(i, i ^ 1) for i in range(devices)]
    caches = (
        cached_keys,
        cached_values,
        lax.ppermute(cached_keys, axes, siblings),
        lax.ppermute(cached_values, axes, siblings),
    )
    message = pack(queries, shard_hits, devices)
    received = lax.all_to_all(message, axes, 0, 0)
    partial = attend(received, caches)
    received = lax.all_to_all(partial, axes, 0, 0)
    return finish(received, *queries.shape)


def solution(mesh):
    both = P(("shard", "seq"), None)
    cache = P("shard", "seq", None)
    return jax.shard_map(
        functools.partial(shards, mesh.size),
        mesh=mesh,
        in_specs=(both, cache, cache, both),
        out_specs=both,
        check_vma=False,
    )
```

```python
import functools
import math

import jax
import jax.numpy as jnp
from jax import lax
from jax.experimental import pallas as pl
from jax.experimental.pallas import tpu as pltpu
from jax.sharding import PartitionSpec as P

HD = 128
KB = 512
LANES = 128
NEG_FILL = -1e30
TO_LOG2 = math.log2(math.e) / math.sqrt(HD)
PACK_COST = 20_000_000_000
VMEM_LIMIT = 24 * 1024 * 1024
PART = 32
SUBLANES = 8


def params():
    return pltpu.CompilerParams(vmem_limit_bytes=VMEM_LIMIT)


def lane_iota(shape):
    return lax.broadcasted_iota(jnp.int32, shape, len(shape) - 1)


def one_hot(condition):
    return jnp.where(condition, 1.0, 0.0).astype(jnp.bfloat16)


def dot(a, b):
    return jnp.dot(a, b, preferred_element_type=jnp.float32)


def parts_of(x, count):
    parts = []
    for _ in range(count):
        part = x.astype(jnp.bfloat16)
        parts.append(part)
        x = x - part.astype(jnp.float32)
    return parts


def pack_body(x_ref, out_ref):
    half = (x_ref.shape[1] - LANES) // 2
    x = x_ref[...]
    for core in range(2):
        message = jnp.concatenate([x[:, core * half:(core + 1) * half], x[:, 2 * half:]], axis=1)
        out_ref[:, core] = jnp.broadcast_to(message[None], (out_ref.shape[0],) + message.shape)


def pack(queries, hits, devices):
    own_rows, width = queries.shape
    listed = jnp.pad(hits, ((0, 0), (width, LANES - hits.shape[1]))) > 0
    joined = jnp.where(listed, 1.0, jnp.pad(queries, ((0, 0), (0, LANES)))).astype(queries.dtype)
    shape = (devices // 2, 2, own_rows, width // 2 + LANES)
    out = pl.pallas_call(
        pack_body,
        out_shape=jax.ShapeDtypeStruct(shape, jnp.bfloat16),
        compiler_params=params(),
        cost_estimate=pl.CostEstimate(flops=PACK_COST, bytes_accessed=0, transcendentals=0),
        name="pack_queries",
    )(joined)
    return out.reshape(devices, own_rows, width // 2 + LANES)


def attend_body(x_ref, *refs):
    *caches, out_ref, q_buf, y_buf = refs
    devices, own_rows, message = x_ref.shape
    width = message - LANES
    heads = width // HD
    local_shards, positions, cache_width = caches[0].shape
    kv_heads = cache_width // HD // 2
    group = heads // kv_heads
    blocks = positions // KB
    rows = devices * own_rows
    cap = rows // 2
    packed = group * cap
    first_column = lax.rem(lax.axis_index("seq"), 2) * (kv_heads * HD)

    x = x_ref[...].reshape(rows, message)
    listed = x[:, width:].astype(jnp.float32)
    first = lax.axis_index("shard") * local_shards
    lane = lane_iota((rows, LANES))
    slots = pltpu.roll(listed, lax.rem(LANES - first, LANES), 1)
    hits = [slots[:, slot:slot + 1] > 0.0 for slot in range(local_shards)]
    row = lax.broadcasted_iota(jnp.int32, (rows, rows), 0)
    column = lax.broadcasted_iota(jnp.int32, (rows, rows), 1)
    place = dot(one_hot(column < row), slots.astype(jnp.bfloat16))
    slots_t = jnp.transpose(slots)[:SUBLANES]
    place_t = dot(slots_t.astype(jnp.bfloat16), one_hot(row < column))

    pick_at = lax.broadcasted_iota(jnp.int32, (cap, rows), 0).astype(jnp.float32)
    picks, backs = [], []
    for slot in range(local_shards):
        picks.append(
            one_hot((pick_at == place_t[slot:slot + 1]) & (slots_t[slot:slot + 1] > 0.0))
        )
        back_at = lax.rem(lane_iota((rows, 3 * cap)), cap).astype(jnp.float32)
        backs.append(one_hot((back_at == place[:, slot:slot + 1]) & hits[slot]))

    mine = pl.ds(pl.multiple_of(first_column, HD), kv_heads * HD)
    caches = [ref.at[:, :, mine] for ref in caches]
    picked = dot(jnp.concatenate(picks, axis=0), x[:, :width]).astype(jnp.bfloat16)
    for slot in range(local_shards):
        q_buf[slot] = picked[slot * cap:(slot + 1) * cap]
    ones = jnp.ones((KB, LANES), jnp.bfloat16)
    cap_lane = lane_iota((cap, LANES))
    levels = [jnp.zeros((cap, LANES), jnp.float32) for _ in range(local_shards)]
    for g in range(kv_heads):
        for slot in range(local_shards):
            level = levels[slot]
            columns = slice(g * HD, (g + 1) * HD)
            group_heads = [g * group + r for r in range(group)]
            query = jnp.concatenate(
                [q_buf[slot, :, h * HD:(h + 1) * HD] for h in group_heads], axis=0
            )
            peaks, sums = [], []
            for block in range(2 * blocks):
                k_ref, v_ref = caches[2 * (block // blocks):2 * (block // blocks) + 2]
                at = slice(block % blocks * KB, (block % blocks + 1) * KB)
                scores = lax.dot_general(
                    k_ref[slot, at, columns], query, (((1,), (1,)), ((), ())),
                    preferred_element_type=jnp.float32,
                )
                peak = jnp.max(scores, axis=0, keepdims=True)
                weights = jnp.exp2((scores - peak) * TO_LOG2).astype(jnp.bfloat16)
                values = jnp.concatenate([v_ref[slot, at, columns], ones], axis=1)
                sums.append(
                    lax.dot_general(
                        weights, values, (((0,), (0,)), ((), ())),
                        preferred_element_type=jnp.float32,
                    )
                )
                peaks.append(peak * TO_LOG2)
            top = functools.reduce(jnp.maximum, peaks)
            factors = [top] + [jnp.exp2(peak - top) for peak in peaks]
            factors.append(jnp.zeros((SUBLANES - len(factors), packed), jnp.float32))
            factors = jnp.transpose(jnp.concatenate(factors, axis=0))
            spread = [
                jnp.broadcast_to(factors[:, i + 1:i + 2], (packed, HD)) for i in range(len(sums))
            ]
            total = sum(
                part * jnp.concatenate([factor] * 2, axis=1) for part, factor in zip(sums, spread)
            )
            average = total[:, :HD] * pl.reciprocal(total[:, HD:])
            log_total = factors[:, :1] + jnp.log2(total[:, HD:])
            for r, h in enumerate(group_heads):
                at = slice(r * cap, (r + 1) * cap)
                y_buf[slot, :, h * HD:(h + 1) * HD] = average[at]
                level = jnp.where(cap_lane == h, log_total[at], level)
            levels[slot] = level

    level_of = []
    for slot in range(local_shards):
        level = dot(backs[slot], jnp.concatenate(parts_of(levels[slot], 3), axis=0))
        level_of.append(jnp.where(hits[slot], level, NEG_FILL))
    top = functools.reduce(jnp.maximum, level_of)
    shares = [
        jnp.where(hit, jnp.exp2(level - top), 0.0) for hit, level in zip(hits, level_of)
    ]
    share_sum = sum(shares)
    some = share_sum > 0.0
    share_sum = jnp.where(some, share_sum, 1.0)
    merged_level = jnp.where(some, top + jnp.log2(share_sum), NEG_FILL)
    scaled = []
    for slot in range(local_shards):
        share = sum(dot(picks[slot], part) for part in parts_of(shares[slot] / share_sum, 2))
        columns = [
            y_buf[slot, :, h * HD:(h + 1) * HD] * share[:, h:h + 1] for h in range(heads)
        ]
        scaled += parts_of(jnp.concatenate(columns, axis=1), 2)
    back_at = lane_iota((rows, 2 * local_shards * cap))
    back_place = lax.rem(back_at, cap).astype(jnp.float32)
    back_slot = lax.div(back_at, 2 * cap)
    back = functools.reduce(
        jnp.logical_or,
        [
            (back_slot == slot) & (back_place == place[:, slot:slot + 1]) & hits[slot]
            for slot in range(local_shards)
        ],
    )
    merged = dot(one_hot(back), jnp.concatenate(scaled, axis=0))
    stats = jnp.zeros((rows, LANES), jnp.float32)
    level_parts = parts_of(jnp.where(lane < heads, merged_level, 0.0), 3)
    for i, part in enumerate(level_parts):
        part = part.astype(jnp.float32)
        stats = stats + (pltpu.roll(part, PART * i, 1) if i else part)
    out = jnp.concatenate([merged, stats], axis=1).astype(jnp.bfloat16)
    out_ref[...] = out.reshape(out_ref.shape)


def attend(message, caches):
    devices, own_rows, columns = message.shape
    keys = caches[0]
    local_shards = keys.shape[0]
    cap = devices * own_rows // 2
    width = columns - LANES
    scores = 2 * cap * width // HD * local_shards * keys.shape[1]
    return pl.pallas_call(
        attend_body,
        out_shape=jax.ShapeDtypeStruct(message.shape, jnp.bfloat16),
        scratch_shapes=[
            pltpu.VMEM((local_shards, cap, width), jnp.bfloat16),
            pltpu.VMEM((local_shards, cap, width), jnp.float32),
        ],
        compiler_params=params(),
        cost_estimate=pl.CostEstimate(
            flops=4 * scores * HD, bytes_accessed=4 * keys.size, transcendentals=scores
        ),
        name="attend",
    )(message, *caches)


def finish_body(x_ref, out_ref):
    devices, own_rows, message = x_ref.shape
    width = message - LANES
    heads = width // HD
    rows = devices * own_rows
    period = 2 * own_rows

    def over_chips(x, combine):
        x = functools.reduce(combine, [x[i] for i in range(x.shape[0])])
        shift = period
        while shift < SUBLANES:
            x = combine(x, pltpu.roll(x, shift, 0))
            shift *= 2
        return x

    x = x_ref[...].reshape(rows, message)
    stats = x[:, width:].astype(jnp.float32)
    top = over_chips(stats.reshape(rows // SUBLANES, SUBLANES, LANES), jnp.maximum)[None]
    level = stats
    for i in (1, 2):
        level = level + pltpu.roll(stats, LANES - PART * i, 1)
    level = level.reshape(rows // SUBLANES, SUBLANES, LANES)
    factor = jnp.where(lane_iota(level.shape) < heads, jnp.exp2(level - top), 0.0)
    total = over_chips(factor, jnp.add)[None]
    share = factor * pl.reciprocal(jnp.where(total > 0.0, total, 1.0))
    share = jnp.transpose(share.reshape(rows, LANES))[:heads]
    high, low = parts_of(share, 2)
    target = lax.broadcasted_iota(jnp.int32, (SUBLANES, rows), 0)
    source = lax.broadcasted_iota(jnp.int32, (SUBLANES, rows), 1)
    mine = target == lax.rem(source, period)
    high, low = high.astype(jnp.float32), low.astype(jnp.float32)
    pieces = []
    for pair in range(0, heads, 2):
        weights = jnp.concatenate(
            [
                jnp.where(mine, part[h:h + 1], 0.0)
                for h in (pair, pair + 1)
                for part in (high, low)
            ],
            axis=0,
        ).astype(jnp.bfloat16)
        both = dot(weights, x[:, pair * HD:(pair + 2) * HD])
        for i in range(2):
            part = both[2 * i * SUBLANES:2 * (i + 1) * SUBLANES, i * HD:(i + 1) * HD]
            pieces.append(part[:SUBLANES] + part[SUBLANES:])
    merged = jnp.concatenate(pieces, axis=1)
    out_ref[...] = jnp.concatenate(
        [merged[core * own_rows:(core + 1) * own_rows] for core in range(2)], axis=1
    ).astype(jnp.bfloat16)


def finish(received, own_rows, width):
    return pl.pallas_call(
        finish_body,
        out_shape=jax.ShapeDtypeStruct((own_rows, width), jnp.bfloat16),
        compiler_params=params(),
        name="finish",
    )(received)


def shards(devices, queries, cached_keys, cached_values, shard_hits):
    axes = ("shard", "seq")
    siblings = [(i, i ^ 1) for i in range(devices)]
    caches = (
        cached_keys,
        cached_values,
        lax.ppermute(cached_keys, axes, siblings),
        lax.ppermute(cached_values, axes, siblings),
    )
    message = pack(queries, shard_hits, devices)
    received = lax.all_to_all(message, axes, 0, 0)
    partial = attend(received, caches)
    received = lax.all_to_all(partial, axes, 0, 0)
    return finish(received, *queries.shape)


def solution(mesh):
    both = P(("shard", "seq"), None)
    cache = P("shard", "seq", None)
    return jax.shard_map(
        functools.partial(shards, mesh.size),
        mesh=mesh,
        in_specs=(both, cache, cache, both),
        out_specs=both,
        check_vma=False,
    )
```
